32 devices in a mesh: genes: 16 (over z, y, x), batch: 2 (over core).
Axes of the slice: x: 2, y: 2, z: 4, core: 2. Of those that a mesh axis runs over, the one named last changes fastest.
Arguments:
- genotypes: bfloat16 [256, 786432], P('batch', 'genes'), may hold values from 0 to 2, as said below
- gene_weight: bfloat16 [16, 786432], P(None, 'genes'), may hold values from -0.375 to 0.375
- gene_lengths: int32 [3072], P('genes'), may hold values from 128 to 384, as said below
- membership: int32 [3072, 2], replicated, may hold values from 0 to 511, as said below
- pathway_slot: int32 [512], replicated, may hold values from 0 to 511, as said below
- pathway_weight: bfloat16 [6144, 1024], P('genes'), may hold values from -0.4375 to 0.4375
- head_weight: bfloat16 [32768], P('genes'), may hold values from -0.75 to 0.75
- cotangent: float32 [256], P('batch'), may hold values from -3 to 3
Outputs:
- grad_gene: float32 [16, 786432], P(None, 'genes')
- grad_pathway: float32 [6144, 1024], P('genes')
- grad_head: float32 [32768], P('genes')
The draws below stay inside these ranges and needn't reach their ends.
Inputs may be any that keep to these rules, and one draw needn't show every extreme that they name: `genotypes`: dosages 0, 1 or 2. `gene_lengths`: the 192 genes of each index of genes together hold exactly its 49152 variants. `membership`: the 2 pathways of a gene differ; of the links of one index's genes at most 48 go to pathways whose slots lie in one index's range of 32 slots, and some index receives exactly 48 from every index. `pathway_slot`: a permutation of the pathways; slot s is held by index s // 32 of genes.
All inputs are finite; a program needn't handle non-finite values.
Results may differ from the reference program's by a relative error of at most 0.0062.
Values may be sent and summed in bfloat16 or wider, within the bound.
No kernel may reach another device: no remote copies, remote signals or barrier semaphores. Data moves between devices by JAX's collectives and lax.ppermute only.
A program may use at most 128 MiB of HBM per device.

```python
import math
import jax
import jax.numpy as jnp
from jax import lax

UNITS = 16
PUNITS = 64
MEMB = 2
GLEN = 256
GENE_DEV = 192
PATH_DEV = 32
SUBJECT_TOTAL = 256
GENES = 3072
VAR_DEV = 49152
VARIANTS = 786432
EDGES_PER_SHARD = 384
EDGES = 6144
PATHWAYS = 512
CAP = 48
N_GENES = 16


def draw_genotypes(key, part):
    freq_key = jax.random.fold_in(key, 1)
    pick_key = jax.random.fold_in(key, 2)
    minor_variant_share = jnp.exp(jax.random.uniform(freq_key, (1, VARIANTS), jnp.float32, math.log(0.03), math.log(0.5)))
    stochastic_uniform_values = jax.random.uniform(pick_key, (SUBJECT_TOTAL, VARIANTS), jnp.float32)
    holds_variant_flag = 1.0 - (1.0 - minor_variant_share) * (1.0 - minor_variant_share)
    variant_copies_matrix = (stochastic_uniform_values < holds_variant_flag).astype(jnp.float32) + (stochastic_uniform_values < minor_variant_share * minor_variant_share).astype(jnp.float32)
    return variant_copies_matrix.astype(jnp.bfloat16)


def draw_gene_lengths(key, part):
    device_count = GENES // GENE_DEV
    half_count = GENE_DEV // 2
    shift = jax.random.randint(jax.random.fold_in(key, 3), (device_count, half_count), -(GLEN // 2), GLEN // 2 + 1)
    shift = shift.at[:, 0].set(GLEN // 2)
    paired = jnp.concatenate([GLEN + shift, GLEN - shift], axis=1)
    scores = jax.random.randint(jax.random.fold_in(key, 4), (device_count, GENE_DEV), 0, 1 << 20) * GENE_DEV
    scores = scores + jnp.arange(GENE_DEV)[None, :]
    order = jnp.argsort(scores, axis=1)
    shuffled = jnp.take_along_axis(paired, order, axis=1)
    return shuffled.reshape(GENES).astype(jnp.int32)


def pathway_lookup(key):
    device_count = GENES // GENE_DEV
    slot_of = jax.random.permutation(jax.random.fold_in(key, 7), PATHWAYS).astype(jnp.int32)
    path_of = jnp.argsort(slot_of).astype(jnp.int32)
    hot_owner = jax.random.randint(jax.random.fold_in(key, 8), (), 0, device_count).astype(jnp.int32)

    def one_device(index):
        device_key = jax.random.fold_in(jax.random.fold_in(key, 9), index)
        cells = jnp.arange(device_count * CAP, dtype=jnp.int32)
        owners = cells // CAP
        scores = jax.random.permutation(jax.random.fold_in(device_key, 1), device_count * CAP).astype(jnp.int32)
        scores = scores + jnp.where(owners == hot_owner, device_count * CAP, 0).astype(jnp.int32)
        chosen = owners[jnp.argsort(scores)][:EDGES_PER_SHARD - CAP]
        targets = jnp.concatenate([jnp.full((CAP,), hot_owner, jnp.int32), chosen.astype(jnp.int32)])
        targets = targets[jax.random.permutation(jax.random.fold_in(device_key, 2), EDGES_PER_SHARD)]
        targets = targets.reshape(GENE_DEV, MEMB)
        first_local = jax.random.randint(jax.random.fold_in(device_key, 3), (GENE_DEV, 1), 0, PATH_DEV)
        step_local = jax.random.randint(jax.random.fold_in(device_key, 4), (GENE_DEV, 1), 1, PATH_DEV)
        local_index = jnp.concatenate([first_local, (first_local + step_local) % PATH_DEV], axis=1)
        return (targets * PATH_DEV + local_index).astype(jnp.int32)
    slots = jax.vmap(one_device)(jnp.arange(device_count, dtype=jnp.int32)).reshape(GENES, MEMB)
    return (slot_of, path_of[slots])


def draw_membership(key, part):
    return pathway_lookup(key)[1]


def draw_pathway_slot(key, part):
    return pathway_lookup(key)[0]


def steps_of(stream_key, shape, split, low, high):
    def one(dim, blocks):
        draws = jax.random.uniform(jax.random.fold_in(jax.random.fold_in(stream_key, 6), dim), (blocks,), jnp.float32, low / len(split), high / len(split))
        return jnp.repeat(jnp.exp(draws), shape[dim] // blocks).reshape((-1,) + (1,) * (len(shape) - dim - 1))

    loudness = one(*split[0])
    for cut in split[1:]:
        loudness = loudness * one(*cut)
    return loudness


def centred(rng, shape, width, bound, cuts=(), kind=jnp.bfloat16):
    drawn = width * jax.random.normal(rng, shape, jnp.float32)
    if cuts:
        drawn = drawn * steps_of(rng, shape, cuts, -0.22, 0.18)
    return jnp.clip(drawn, -bound, bound).astype(kind)


def setup_inputs(seed: int = 0) -> dict:
    key_of = jax.random.split(jax.random.key(seed), 9)
    return {
        "genotypes": draw_genotypes(jax.random.fold_in(key_of[8], 71), 0),
        "gene_weight": centred(key_of[1], (UNITS, VARIANTS), GLEN ** -0.5, 0.375, ((1, 16),)),
        "gene_lengths": draw_gene_lengths(jax.random.fold_in(key_of[8], 71), 0),
        "membership": draw_membership(jax.random.fold_in(key_of[8], 71), 0),
        "pathway_slot": draw_pathway_slot(jax.random.fold_in(key_of[8], 71), 0),
        "pathway_weight": centred(key_of[5], (EDGES, UNITS * PUNITS), 192 ** -0.5, 0.4375, ((0, 16),)),
        "head_weight": centred(key_of[6], (PATHWAYS * PUNITS,), PUNITS ** -0.5, 0.75, ((0, 16),)),
        "cotangent": centred(key_of[7], (SUBJECT_TOTAL,), 0.5, 3.0, ((0, 2),), jnp.float32),
    }


block_cols = 512


def gene_window_count():
    return block_cols // (GLEN // 2) + 2


def gene_windows(lengths, var_count, window):
    starts = (jnp.cumsum(lengths) - lengths).astype(jnp.int32)
    blocks = var_count // block_cols
    block_start = (jnp.arange(blocks) * block_cols).astype(jnp.int32)
    first_gene = (jnp.sum((starts[None, :] <= block_start[:, None]).astype(jnp.int32), axis=1) - 1).astype(jnp.int32)
    padded = jnp.concatenate([starts, jnp.full((window,), var_count, jnp.int32)])
    upcoming = padded[first_gene[:, None] + jnp.arange(1, window, dtype=jnp.int32)[None, :]]
    position = block_start[:, None] + jnp.arange(block_cols, dtype=jnp.int32)[None, :]
    which = jnp.sum((upcoming[:, None, :] <= position[:, :, None]).astype(jnp.int32), axis=2).astype(jnp.int32)
    select = which[:, None, :] == jnp.arange(window, dtype=jnp.int32)[None, :, None]
    gene_ids = first_gene[:, None] + jnp.arange(window, dtype=jnp.int32)[None, :]
    return gene_ids, select


def gene_forward(genotype_rows, weight_rows, lengths):
    samples, var_count = genotype_rows.shape
    unit_count = weight_rows.shape[0]
    window_genes = gene_window_count()
    gene_ids, select = gene_windows(lengths, var_count, window_genes)
    blocks = var_count // block_cols
    rows = genotype_rows.astype(jnp.float32).reshape(samples, blocks, block_cols)
    weight_blocks = weight_rows.astype(jnp.float32).reshape(unit_count, blocks, block_cols).transpose(1, 0, 2)
    basis = jnp.where(select[:, :, None, :], weight_blocks[:, None, :, :], jnp.zeros((), jnp.float32))
    basis = basis.reshape(blocks, window_genes * unit_count, block_cols)
    partial_sums = jnp.einsum("bkv,kcv->kcb", rows, basis)
    partial_sums = partial_sums.reshape(blocks * window_genes, unit_count, samples)
    preact = jax.ops.segment_sum(partial_sums, gene_ids.reshape(-1), num_segments=lengths.shape[0])
    return preact, gene_ids, select


def gene_backward(genotype_rows, preact_delta, gene_ids, select):
    samples, var_count = genotype_rows.shape
    gene_count, unit_count, _ = preact_delta.shape
    blocks = var_count // block_cols
    window = gene_ids.shape[1]
    rows = genotype_rows.astype(jnp.float32).reshape(samples, blocks, block_cols)
    windowed = preact_delta[jnp.minimum(gene_ids, gene_count - 1)].astype(jnp.float32)
    windowed = windowed.reshape(blocks, window * unit_count, samples)
    full_terms = jnp.einsum("bkv,kcb->kcv", rows, windowed).reshape(blocks, window, unit_count, block_cols)
    selected_entries = jnp.sum(jnp.where(select[:, :, None, :], full_terms, jnp.zeros((), jnp.float32)), axis=1)
    return selected_entries.transpose(1, 0, 2).reshape(unit_count, var_count)


def reference(genotypes, gene_weight, gene_lengths, membership, pathway_slot, pathway_weight, head_weight, cotangent):
    unit_count = gene_weight.shape[0]
    slots = pathway_slot[membership].astype(jnp.int32).reshape(-1)
    head_rows = head_weight.astype(jnp.float32).reshape(PATHWAYS, -1)
    path_units = head_rows.shape[1]
    link_weights = pathway_weight.reshape(EDGES, unit_count, path_units)
    shard_ids = jnp.arange(N_GENES, dtype=jnp.int32)

    def shard_inputs(index):
        rows = lax.dynamic_slice_in_dim(genotypes, index * VAR_DEV, VAR_DEV, 1)
        weight_rows = lax.dynamic_slice_in_dim(gene_weight, index * VAR_DEV, VAR_DEV, 1)
        lengths = lax.dynamic_slice_in_dim(gene_lengths, index * GENE_DEV, GENE_DEV, 0)
        link_rows = lax.dynamic_slice_in_dim(link_weights, index * EDGES_PER_SHARD, EDGES_PER_SHARD, 0)
        own_slots = lax.dynamic_slice_in_dim(slots, index * EDGES_PER_SHARD, EDGES_PER_SHARD, 0)
        return rows, weight_rows, lengths, link_rows, own_slots

    def forward_shard(totals, index):
        rows, weight_rows, lengths, link_rows, own_slots = shard_inputs(index)
        preact, gene_ids, select = gene_forward(rows, weight_rows, lengths)
        hidden = jnp.tanh(preact).astype(jnp.bfloat16)
        hidden_links = jnp.repeat(hidden, MEMB, axis=0).astype(jnp.float32)
        message = jnp.einsum("eub,euk->ekb", hidden_links, link_rows.astype(jnp.float32)).astype(jnp.bfloat16)
        message = lax.optimization_barrier(message).astype(jnp.float32)
        totals = totals + jax.ops.segment_sum(message, own_slots, num_segments=PATHWAYS)
        return totals, hidden

    start_sums = jnp.zeros((PATHWAYS, path_units, SUBJECT_TOTAL), jnp.float32)
    pathway_sum, hiddens = lax.scan(forward_shard, start_sums, shard_ids)
    active = jnp.tanh(pathway_sum)
    grad_head = jnp.sum(active * cotangent[None, None, :], axis=2).reshape(-1)
    pathway_delta = (cotangent[None, None, :] * head_rows[:, :, None] * (1.0 - active * active)).astype(jnp.bfloat16)

    def backward_shard(carry, inputs):
        index, hidden = inputs
        rows, weight_rows, lengths, link_rows, own_slots = shard_inputs(index)
        gene_ids, select = gene_windows(lengths, VAR_DEV, gene_window_count())
        link_delta_rows = pathway_delta[own_slots].astype(jnp.float32)
        hidden_links = jnp.repeat(hidden, MEMB, axis=0).astype(jnp.float32)
        grad_links = jnp.einsum("eub,ekb->euk", hidden_links, link_delta_rows).reshape(EDGES_PER_SHARD, -1)
        hidden_delta = jnp.einsum("euk,ekb->eub", link_rows.astype(jnp.float32), link_delta_rows)
        hidden_delta = jnp.sum(hidden_delta.reshape(GENE_DEV, MEMB, unit_count, SUBJECT_TOTAL), axis=1)
        latent_broad_matrix = hidden.astype(jnp.float32)
        preact_delta = (hidden_delta * (1.0 - latent_broad_matrix * latent_broad_matrix)).astype(jnp.bfloat16)
        grad_rows = gene_backward(rows, preact_delta, gene_ids, select)
        return carry, (grad_rows, grad_links)

    _, (gene_grads, link_grads) = lax.scan(backward_shard, jnp.zeros((), jnp.float32), (shard_ids, hiddens))
    grad_gene = gene_grads.transpose(1, 0, 2).reshape(unit_count, VARIANTS)
    grad_pathway = link_grads.reshape(EDGES, -1)
    return grad_gene, grad_pathway, grad_head
```

```python
import functools

import jax
import jax.numpy as jnp
from jax import lax
from jax.experimental import pallas as pl
from jax.experimental.pallas import tpu as pltpu
from jax.sharding import PartitionSpec as P

BLOCK = 512
MIN_GENE = 128
WINDOW = BLOCK // MIN_GENE + 1
GROUP = 4
LANES = 128
ROWS = 16
VMEM_LIMIT = 56 * 1024 * 1024

smem = pl.BlockSpec(memory_space=pltpu.SMEM)
vmem = pl.BlockSpec(memory_space=pltpu.VMEM)


def nt_dot(left, right):
    return lax.dot_general(
        left, right, (((1,), (1,)), ((), ())), preferred_element_type=jnp.float32
    )


def nn_dot(left, right):
    return jnp.dot(left, right, preferred_element_type=jnp.float32)


def fill_tables(gene_count, var_count, lengths, starts, first):
    def body(gene, start):
        starts[gene] = start
        end = start + lengths[gene]
        block = (start + (BLOCK - 1)) // BLOCK

        @pl.when(block * BLOCK < end)
        def _():
            first[block] = gene

        return end

    lax.fori_loop(0, gene_count, body, jnp.int32(0))
    for extra in range(WINDOW + 1):
        starts[gene_count + extra] = jnp.int32(var_count)


def window_masks(starts, gene, base, rows):
    position = lax.broadcasted_iota(jnp.int32, (rows, BLOCK), 1)
    masks = []
    for j in range(WINDOW):
        low = starts[gene + j] - base
        high = starts[gene + j + 1] - base
        masks.append((position >= low) & (position < high))
    return masks


def gene_forward_kernel(
    gene_count, var_count, blocks, lengths, geno, weight, out, pre, starts, first
):
    step = pl.program_id(0)
    units = weight.shape[0]

    @pl.when(step == 0)
    def _():
        fill_tables(gene_count, var_count, lengths, starts, first)
        pre[...] = jnp.zeros_like(pre)

    for i in range(blocks):
        block = step * blocks + i
        gene = first[block]
        masks = window_masks(starts, gene, block * BLOCK, units)
        wide = weight[:, i * BLOCK : (i + 1) * BLOCK].astype(jnp.float32)
        basis = jnp.concatenate(
            [jnp.where(mask, wide, 0.0).astype(jnp.bfloat16) for mask in masks], axis=0
        )
        part = nt_dot(basis, geno[:, i * BLOCK : (i + 1) * BLOCK])
        where = pl.ds(pl.multiple_of(gene * units, units), WINDOW * units)
        pre[where, :] += part

    @pl.when(step == pl.num_programs(0) - 1)
    def _():
        def body(i, _):
            at = pl.multiple_of(i * LANES, LANES)
            tile = jnp.tanh(pre[pl.ds(at, LANES), :])
            out[:, pl.ds(at, LANES)] = tile.T.astype(jnp.bfloat16)
            return 0

        lax.fori_loop(0, gene_count * units // LANES, body, 0, unroll=4)


def gene_forward(genotypes, gene_weight, lengths):
    samples, var_count = genotypes.shape
    units = gene_weight.shape[0]
    gene_count = lengths.shape[0]
    total = var_count // BLOCK
    blocks = next(n for n in (8, 4, 2, 1) if total % n == 0)
    cols = blocks * BLOCK
    return pl.pallas_call(
        functools.partial(gene_forward_kernel, gene_count, var_count, blocks),
        out_shape=jax.ShapeDtypeStruct((samples, gene_count * units), jnp.bfloat16),
        grid=(total // blocks,),
        in_specs=[
            smem,
            pl.BlockSpec((samples, cols), lambda i: (0, i)),
            pl.BlockSpec((units, cols), lambda i: (0, i)),
        ],
        out_specs=pl.BlockSpec((samples, gene_count * units), lambda i: (0, 0)),
        scratch_shapes=[
            pltpu.VMEM(((gene_count + WINDOW) * units, samples), jnp.float32),
            pltpu.SMEM((gene_count + WINDOW + 1,), jnp.int32),
            pltpu.SMEM((total,), jnp.int32),
        ],
        compiler_params=pltpu.CompilerParams(vmem_limit_bytes=VMEM_LIMIT),
        cost_estimate=pl.CostEstimate(
            flops=2 * WINDOW * units * samples * var_count,
            bytes_accessed=2 * (samples + units) * var_count,
            transcendentals=gene_count * units * samples,
        ),
        name="gene_forward",
    )(lengths, genotypes, gene_weight)


def gene_backward_kernel(
    gene_count, var_count, blocks, lengths, geno, delta, out, rows, starts, first
):
    step = pl.program_id(0)
    units = out.shape[0]

    @pl.when(step == 0)
    def _():
        fill_tables(gene_count, var_count, lengths, starts, first)
        tail = WINDOW * units
        rows[gene_count * units :, :] = jnp.zeros((tail, rows.shape[1]), rows.dtype)

        def body(i, _):
            at = pl.multiple_of(i * LANES, LANES)
            tile = delta[:, pl.ds(at, LANES)].astype(jnp.float32)
            rows[pl.ds(at, LANES), :] = tile.T.astype(jnp.bfloat16)
            return 0

        lax.fori_loop(0, gene_count * units // LANES, body, 0, unroll=4)

    for i in range(blocks):
        block = step * blocks + i
        gene = first[block]
        masks = window_masks(starts, gene, block * BLOCK, units)
        where = pl.ds(pl.multiple_of(gene * units, units), WINDOW * units)
        terms = nn_dot(rows[where, :], geno[:, i * BLOCK : (i + 1) * BLOCK])
        total = jnp.where(masks[0], terms[:units], 0.0)
        for j in range(1, WINDOW):
            total = jnp.where(masks[j], terms[j * units : (j + 1) * units], total)
        out[:, i * BLOCK : (i + 1) * BLOCK] = total.astype(out.dtype)


def gene_backward(genotypes, delta, lengths, units):
    samples, var_count = genotypes.shape
    gene_count = lengths.shape[0]
    total = var_count // BLOCK
    blocks = next(n for n in (8, 4, 2, 1) if total % n == 0)
    cols = blocks * BLOCK
    return pl.pallas_call(
        functools.partial(gene_backward_kernel, gene_count, var_count, blocks),
        out_shape=jax.ShapeDtypeStruct((units, var_count), jnp.bfloat16),
        grid=(total // blocks,),
        in_specs=[
            smem,
            pl.BlockSpec((samples, cols), lambda i: (0, i)),
            pl.BlockSpec((samples, gene_count * units), lambda i: (0, 0)),
        ],
        out_specs=pl.BlockSpec((units, cols), lambda i: (0, i)),
        scratch_shapes=[
            pltpu.VMEM(((gene_count + WINDOW) * units, samples), jnp.bfloat16),
            pltpu.SMEM((gene_count + WINDOW + 1,), jnp.int32),
            pltpu.SMEM((total,), jnp.int32),
        ],
        compiler_params=pltpu.CompilerParams(vmem_limit_bytes=VMEM_LIMIT),
        cost_estimate=pl.CostEstimate(
            flops=2 * WINDOW * units * samples * var_count,
            bytes_accessed=2 * (samples + units) * var_count,
            transcendentals=0,
        ),
        name="gene_backward",
    )(lengths, genotypes, delta)


def lane_groups(dtype, rows, width):
    lane = lax.broadcasted_iota(jnp.int32, (rows, LANES), 1) // width
    return [(lane == r).astype(jnp.float32).astype(dtype) for r in range(LANES // width)]


def swap_halves(x):
    half = LANES // 2
    return jnp.concatenate([x[:, half:], x[:, :half]], axis=1)


def link_forward_kernel(half_genes, units, place, members, slots, hidden, *refs):
    weights, outs, sums = refs[: 2 * GROUP], refs[2 * GROUP : -2], refs[-2:]
    quarter, core = place[0], place[1]
    tiles = LANES // units
    for total in sums:
        total[...] = jnp.zeros_like(total)
    keep = lane_groups(jnp.bfloat16, ROWS, units)
    low, high = lane_groups(jnp.bfloat16, LANES, LANES // 2)
    for piece in range(2 * GROUP):
        source = quarter ^ (piece % GROUP)
        half = core ^ (piece // GROUP)

        def body(t, _, piece=piece, source=source, half=half):
            first = half * half_genes + t * tiles
            at = pl.multiple_of(first * units, LANES)
            own = hidden[source, :, pl.ds(at, LANES)]
            upper, lower = own[:ROWS], own[ROWS:]
            left = jnp.concatenate(
                [jnp.concatenate([upper * k, lower * k], axis=1) for k in keep], axis=0
            )
            block = weights[piece][pl.ds(pl.multiple_of(t * LANES, LANES), LANES), :]
            turned = swap_halves(block)
            right = jnp.concatenate(
                [
                    jnp.concatenate([block * low, turned * low], axis=1),
                    jnp.concatenate([turned * high, block * high], axis=1),
                ],
                axis=0,
            )
            message = nn_dot(left, right)
            gene = source * (2 * half_genes) + first
            for r in range(tiles):
                for m in range(2):
                    slot = slots[members[m, gene + r]]
                    sums[m][slot] += message[
                        r * ROWS : (r + 1) * ROWS, m * LANES : (m + 1) * LANES
                    ]
            return 0

        lax.fori_loop(0, half_genes // tiles, body, 0, unroll=2)
    shard = outs[0].shape[0]
    for i, out in enumerate(outs):
        out[...] = (
            sums[0][i * shard : (i + 1) * shard] + sums[1][i * shard : (i + 1) * shard]
        ).astype(out.dtype)


def link_forward(place, members, slots, hidden, weights, shards):
    units = weights[0].shape[1] // 8
    half_genes = weights[0].shape[0] // units
    slot_count = slots.shape[0]
    out = jax.ShapeDtypeStruct((slot_count // shards, ROWS, LANES), jnp.bfloat16)
    return pl.pallas_call(
        functools.partial(link_forward_kernel, half_genes, units),
        out_shape=[out] * shards,
        in_specs=[smem, smem, smem, vmem] + [vmem] * len(weights),
        out_specs=[vmem] * shards,
        scratch_shapes=[pltpu.VMEM((slot_count, ROWS, LANES), jnp.float32)] * 2,
        compiler_params=pltpu.CompilerParams(vmem_limit_bytes=VMEM_LIMIT),
        cost_estimate=pl.CostEstimate(
            flops=4 * 10**9, bytes_accessed=8 * 10**6, transcendentals=0
        ),
        name="link_forward",
    )(place, members, slots, hidden, *weights)


def link_backward_kernel(half_genes, units, shards, place, members, slots, hidden, *refs):
    weights = refs[: 2 * GROUP]
    deltas = refs[2 * GROUP : 2 * GROUP + shards]
    out, grads, table = refs[2 * GROUP + shards], refs[2 * GROUP + shards + 1 : -1], refs[-1]
    quarter, core = place[0], place[1]
    tiles = LANES // units
    shard = deltas[0].shape[0]
    for i, delta in enumerate(deltas):
        table[i * shard : (i + 1) * shard] = delta[...]
    low, high = lane_groups(jnp.bfloat16, ROWS, LANES // 2)
    samples = hidden.shape[1]
    keep = lane_groups(jnp.float32, samples, units)
    row_gene = lax.broadcasted_iota(jnp.int32, (LANES, LANES), 0) // units
    lane_gene = lax.broadcasted_iota(jnp.int32, (LANES, LANES), 1) // samples
    fits = [
        (row_gene == lane_gene + i * (LANES // samples)).astype(jnp.float32)
        for i in range(tiles * samples // LANES)
    ]
    for piece in range(2 * GROUP):
        source = quarter ^ (piece % GROUP)
        half = core ^ (piece // GROUP)

        def body(t, _, piece=piece, source=source, half=half):
            first = half * half_genes + t * tiles
            at = pl.multiple_of(first * units, LANES)
            here = pl.ds(pl.multiple_of(t * LANES, LANES), LANES)
            own = hidden[source, :, pl.ds(at, LANES)].astype(jnp.float32)
            gene = source * (2 * half_genes) + first
            parts = []
            for r in range(tiles):
                one = table[slots[members[0, gene + r]]]
                two = table[slots[members[1, gene + r]]]
                parts.append(one * low + swap_halves(two) * high)
                parts.append(swap_halves(one) * low + two * high)
            right = jnp.concatenate(parts, axis=0)
            wide = nt_dot(right, weights[piece][here, :])
            back = wide[:samples] * keep[0]
            for r in range(1, tiles):
                back += wide[r * samples : (r + 1) * samples] * keep[r]
            out[source, :, pl.ds(at, LANES)] = (back * (1.0 - own * own)).astype(out.dtype)
            flat = jnp.concatenate([own] * (LANES // samples), axis=0).T
            left = jnp.concatenate([(flat * fit).astype(jnp.bfloat16) for fit in fits], axis=1)
            grads[piece][here, :] = nn_dot(left, right).astype(grads[piece].dtype)
            return 0

        lax.fori_loop(0, half_genes // tiles, body, 0, unroll=2)


def link_backward(place, members, slots, hidden, weights, deltas):
    units = weights[0].shape[1] // 8
    half_genes = weights[0].shape[0] // units
    slot_count = slots.shape[0]
    shards = len(deltas)
    grad = jax.ShapeDtypeStruct(weights[0].shape, jnp.bfloat16)
    return pl.pallas_call(
        functools.partial(link_backward_kernel, half_genes, units, shards),
        out_shape=[jax.ShapeDtypeStruct(hidden.shape, jnp.bfloat16)] + [grad] * len(weights),
        in_specs=[smem, smem, smem, vmem] + [vmem] * (len(weights) + shards),
        out_specs=[vmem] * (1 + len(weights)),
        scratch_shapes=[pltpu.VMEM((slot_count, ROWS, LANES), jnp.bfloat16)],
        compiler_params=pltpu.CompilerParams(vmem_limit_bytes=VMEM_LIMIT),
        cost_estimate=pl.CostEstimate(
            flops=6 * 10**9, bytes_accessed=10 * 10**6, transcendentals=0
        ),
        name="link_backward",
    )(place, members, slots, hidden, *weights, *deltas)


def on_device(
    genotypes,
    gene_weight,
    gene_lengths,
    membership,
    pathway_slot,
    pathway_weight,
    head_weight,
    cotangent,
):
    devices = lax.axis_size("genes")
    index = lax.axis_index("genes")
    core = lax.axis_index("batch")
    planes = devices // GROUP
    plane, quarter = index // GROUP, index % GROUP
    gene_count = gene_lengths.shape[0]
    units = gene_weight.shape[0]
    path_units = pathway_weight.shape[1] // units
    slot_count = pathway_slot.shape[0]
    shard = slot_count // planes
    samples = genotypes.shape[0]
    part = samples // GROUP
    half_rows = gene_count * units // 2
    in_plane = [[GROUP * z + q for q in range(GROUP)] for z in range(planes)]
    along = [[GROUP * z + q for z in range(planes)] for q in range(GROUP)]
    paired = planes == 4

    def swap_plane(x, d):
        pairs = [(GROUP * z + q, GROUP * z + (q ^ d)) for z in range(planes) for q in range(GROUP)]
        return lax.ppermute(x, "genes", pairs)

    def swap_along(x, d):
        pairs = [(GROUP * z + q, GROUP * (z ^ d) + q) for z in range(planes) for q in range(GROUP)]
        return lax.ppermute(x, "genes", pairs)

    def swap_core(x):
        return lax.ppermute(x, "batch", [(0, 1), (1, 0)])

    def spread(x, groups):
        return lax.all_to_all(
            x, "genes", split_axis=0, concat_axis=0, tiled=True, axis_index_groups=groups
        )

    with jax.named_scope("link_weights"):
        folded = pathway_weight.reshape(gene_count, 2, units, path_units)
        folded = folded.transpose(0, 2, 1, 3).reshape(gene_count * units, 2 * path_units)
        mine = lax.dynamic_slice_in_dim(folded, core * half_rows, half_rows)
        other = lax.dynamic_slice_in_dim(folded, (1 - core) * half_rows, half_rows)
        near = [mine] + [swap_plane(mine, d) for d in range(1, GROUP)]
        far = [other] + [swap_core(x) for x in near[1:]]
        weights = near + far

    with jax.named_scope("tables"):
        place = jnp.stack([quarter, core]).astype(jnp.int32)
        members = lax.dynamic_slice_in_dim(
            membership, plane * GROUP * gene_count, GROUP * gene_count
        ).T
        slots = pathway_slot ^ (plane * shard) if paired else pathway_slot
        head = lax.all_gather(
            head_weight, "genes", axis=0, tiled=True, axis_index_groups=in_plane
        )
        head = head.reshape(shard, 1, 1, path_units).astype(jnp.float32)
        cot = lax.dynamic_slice_in_dim(cotangent, quarter * part, part)
        cot = cot.reshape(part // ROWS, ROWS).T.reshape(1, ROWS, part // ROWS, 1)

    with jax.named_scope("hidden"):
        hidden = gene_forward(genotypes, gene_weight, gene_lengths)
        hidden = spread(hidden.reshape(GROUP, part, gene_count * units), in_plane)

    with jax.named_scope("pathway_sum"):
        sums = link_forward(place, members, slots, hidden, weights, planes)
        if paired:
            passed = sums[2].astype(jnp.float32) + swap_along(sums[3], 1).astype(jnp.float32)
            crossed = swap_along(passed.astype(jnp.bfloat16), 2)
            beside = swap_along(sums[1], 1)
            total = (
                sums[0].astype(jnp.float32)
                + crossed.astype(jnp.float32)
                + beside.astype(jnp.float32)
            )
        else:
            parts = spread(jnp.stack(sums), along)
            total = jnp.sum(parts.astype(jnp.float32), axis=0)

    with jax.named_scope("head"):
        total = total.reshape(shard, ROWS, part // ROWS, path_units)
        active = jnp.tanh(total)
        head_part = jnp.sum(active * cot, axis=(1, 2)).reshape(-1)
        delta = (cot * head * (1.0 - active * active)).astype(jnp.bfloat16)
        delta = delta.reshape(shard, ROWS, LANES)

    with jax.named_scope("pathway_delta"):
        if paired:
            one, two = swap_along(delta, 1), swap_along(delta, 2)
            deltas = [delta, one, two, swap_along(two, 1)]
        else:
            every = lax.all_gather(delta, "genes", axis=0, axis_index_groups=along)
            deltas = [every[i] for i in range(planes)]

    with jax.named_scope("link_grads"):
        back, *grads = link_backward(place, members, slots, hidden, weights, deltas)
        back = spread(back, in_plane).reshape(samples, gene_count * units)

    with jax.named_scope("grad_gene"):
        rows = gene_backward(genotypes, back, gene_lengths, units)
        grad_gene = rows.astype(jnp.float32) + swap_core(rows).astype(jnp.float32)

    with jax.named_scope("grad_pathway"):
        summed = [
            keep.astype(jnp.float32) + swap_core(give).astype(jnp.float32)
            for keep, give in zip(grads[:GROUP], grads[GROUP:])
        ]
        own = summed[0]
        for d in range(1, GROUP):
            own = own + swap_plane(summed[d].astype(jnp.bfloat16), d).astype(jnp.float32)
        theirs = swap_core(own)
        first = jnp.where(core == 0, own, theirs)
        second = jnp.where(core == 0, theirs, own)
        links = jnp.concatenate([first, second], axis=0)
        links = links.reshape(gene_count, units, 2, path_units).transpose(0, 2, 1, 3)
        grad_pathway = links.reshape(pathway_weight.shape)

    with jax.named_scope("grad_head"):
        head_part = spread(head_part.reshape(GROUP, -1), in_plane)
        head_part = jnp.sum(head_part, axis=0)
        grad_head = head_part + swap_core(head_part)

    return (grad_gene, grad_pathway, grad_head)


def solution(mesh):
    return jax.shard_map(
        on_device,
        mesh=mesh,
        in_specs=(
            P("batch", "genes"),
            P(None, "genes"),
            P("genes"),
            P(),
            P(),
            P("genes", None),
            P("genes"),
            P("batch"),
        ),
        out_specs=(P(None, "genes"), P("genes", None), P("genes")),
        check_vma=False,
    )
```

```python
import functools

import jax
import jax.numpy as jnp
from jax import lax
from jax.experimental import pallas as pl
from jax.experimental.pallas import tpu as pltpu
from jax.sharding import PartitionSpec as P

BLOCK = 512
MIN_GENE = 128
WINDOW = BLOCK // MIN_GENE + 1
GROUP = 4
LANES = 128
ROWS = 16
SUBLANES = 8
UNROLL = 12
VMEM_LIMIT = 56 * 1024 * 1024

smem = pl.BlockSpec(memory_space=pltpu.SMEM)
vmem = pl.BlockSpec(memory_space=pltpu.VMEM)
hbm = pl.BlockSpec(memory_space=pl.ANY)


def nt_dot(left, right):
    return lax.dot_general(
        left, right, (((1,), (1,)), ((), ())), preferred_element_type=jnp.float32
    )


def nn_dot(left, right):
    return jnp.dot(left, right, preferred_element_type=jnp.float32)


def chunk_blocks(var_count):
    total = var_count // BLOCK
    return next(n for n in (8, 6, 4, 3, 2, 1) if total % n == 0)


def window_edges(lengths, gene_count, gene, start):
    edges = [start]
    for j in range(WINDOW):
        at = gene + j
        length = lengths[jnp.minimum(at, gene_count - 1)]
        edges.append(edges[-1] + jnp.where(at < gene_count, length, 0))
    return edges


def next_window(edges, gene, base):
    start = edges[0]
    for edge in edges[1:]:
        passed = edge <= base
        gene = gene + passed.astype(jnp.int32)
        start = jnp.where(passed, edge, start)
    return gene, start


def reached(edges, base):
    position = lax.broadcasted_iota(jnp.int32, (SUBLANES, BLOCK), 1)
    return [position >= edge - base for edge in edges]


def gene_forward_kernel(
    gene_count, blocks, lengths, geno_hbm, weight_hbm, out, geno, weight, pre, sems
):
    units = weight.shape[0]
    cols = blocks * BLOCK
    chunks = geno.shape[1] // cols

    def copies(c):
        at = pl.ds(pl.multiple_of(c * cols, cols), cols)
        return (
            pltpu.make_async_copy(geno_hbm.at[:, at], geno.at[:, at], sems.at[0, c]),
            pltpu.make_async_copy(weight_hbm.at[:, at], weight.at[:, at], sems.at[1, c]),
        )

    for c in range(chunks):
        for copy in copies(c):
            copy.start()
    pre[...] = jnp.zeros_like(pre)

    def chunk(c, carry):
        gene, start = carry
        for copy in copies(c):
            copy.wait()
        for i in range(blocks):
            base = c * cols + i * BLOCK
            at = pl.ds(pl.multiple_of(base, BLOCK), BLOCK)
            edges = window_edges(lengths, gene_count, gene, start)
            marks = reached(edges, base)
            wide = weight[:, at]
            rows = []
            for j in range(WINDOW):
                mark = (marks[j] & ~marks[j + 1]).astype(jnp.float32)
                mark = jnp.concatenate([mark] * (units // SUBLANES), axis=0)
                rows.append(wide * mark.astype(wide.dtype))
            part = nt_dot(jnp.concatenate(rows, axis=0), geno[:, at])
            where = pl.ds(pl.multiple_of(gene * units, units), WINDOW * units)
            pre[where, :] += part
            gene, start = next_window(edges, gene, base + BLOCK)
        return gene, start

    lax.fori_loop(0, chunks, chunk, (jnp.int32(0), jnp.int32(0)))

    def body(i, _):
        at = pl.multiple_of(i * LANES, LANES)
        tile = jnp.concatenate(
            [pre[pl.ds(at + u, LANES // units, stride=units), :] for u in range(units)], axis=0
        )
        out[:, pl.ds(at, LANES)] = jnp.tanh(tile).T.astype(jnp.bfloat16)
        return 0

    lax.fori_loop(0, gene_count * units // LANES, body, 0, unroll=4)


def gene_forward(genotypes, gene_weight, lengths):
    samples, var_count = genotypes.shape
    units = gene_weight.shape[0]
    gene_count = lengths.shape[0]
    blocks = chunk_blocks(var_count)
    return pl.pallas_call(
        functools.partial(gene_forward_kernel, gene_count, blocks),
        out_shape=jax.ShapeDtypeStruct((samples, gene_count * units), jnp.bfloat16),
        in_specs=[smem, hbm, hbm],
        out_specs=vmem,
        scratch_shapes=[
            pltpu.VMEM(genotypes.shape, jnp.bfloat16),
            pltpu.VMEM(gene_weight.shape, jnp.bfloat16),
            pltpu.VMEM(((gene_count + WINDOW) * units, samples), jnp.float32),
            pltpu.SemaphoreType.DMA((2, var_count // (blocks * BLOCK))),
        ],
        compiler_params=pltpu.CompilerParams(vmem_limit_bytes=VMEM_LIMIT),
        cost_estimate=pl.CostEstimate(
            flops=2 * WINDOW * units * samples * var_count,
            bytes_accessed=2 * (samples + units) * var_count,
            transcendentals=gene_count * units * samples,
        ),
        name="gene_forward",
    )(lengths, genotypes, gene_weight)


def gene_backward_kernel(
    gene_count, blocks, lengths, geno_hbm, delta, out_hbm, geno, out, rows, sems
):
    units = out.shape[0]
    cols = blocks * BLOCK
    chunks = geno.shape[1] // cols

    def chunk_copy(c):
        at = pl.ds(pl.multiple_of(c * cols, cols), cols)
        return pltpu.make_async_copy(geno_hbm.at[:, at], geno.at[:, at], sems.at[0, c])

    def chunk_store(c):
        at = pl.ds(pl.multiple_of(c * cols, cols), cols)
        return pltpu.make_async_copy(out.at[:, at], out_hbm.at[:, at], sems.at[1, c])

    for c in range(chunks):
        chunk_copy(c).start()
    tail = WINDOW * units
    rows[gene_count * units :, :] = jnp.zeros((tail, rows.shape[1]), rows.dtype)

    count = LANES // units

    def body(i, _):
        at = pl.multiple_of(i * LANES, LANES)
        tile = delta[:, pl.ds(at, LANES)].astype(jnp.float32).T
        for u in range(units):
            here = pl.ds(at + u, count, stride=units)
            rows[here, :] = tile[u * count : (u + 1) * count]
        return 0

    lax.fori_loop(0, delta.shape[1] // LANES, body, 0, unroll=4)

    def chunk(c, carry):
        gene, start = carry
        chunk_copy(c).wait()
        for i in range(blocks):
            base = c * cols + i * BLOCK
            at = pl.ds(pl.multiple_of(base, BLOCK), BLOCK)
            edges = window_edges(lengths, gene_count, gene, start)
            marks = reached(edges, base)
            where = pl.ds(pl.multiple_of(gene * units, units), WINDOW * units)
            terms = nn_dot(rows[where, :].astype(jnp.bfloat16), geno[:, at])
            pieces = []
            for u in range(0, units, SUBLANES):
                total = terms[u : u + SUBLANES]
                for j in range(1, WINDOW):
                    here = j * units + u
                    total = jnp.where(marks[j], terms[here : here + SUBLANES], total)
                pieces.append(total)
            out[:, at] = jnp.concatenate(pieces, axis=0).astype(out.dtype)
            gene, start = next_window(edges, gene, base + BLOCK)
        chunk_store(c).start()
        return gene, start

    lax.fori_loop(0, chunks, chunk, (jnp.int32(0), jnp.int32(0)))
    for c in range(chunks):
        chunk_store(c).wait()


def gene_backward(genotypes, delta, lengths, units):
    samples, var_count = genotypes.shape
    gene_count = lengths.shape[0]
    blocks = chunk_blocks(var_count)
    return pl.pallas_call(
        functools.partial(gene_backward_kernel, gene_count, blocks),
        out_shape=jax.ShapeDtypeStruct((units, var_count), jnp.bfloat16),
        in_specs=[smem, hbm, vmem],
        out_specs=hbm,
        scratch_shapes=[
            pltpu.VMEM(genotypes.shape, jnp.bfloat16),
            pltpu.VMEM((units, var_count), jnp.bfloat16),
            pltpu.VMEM(((gene_count + WINDOW) * units, samples), jnp.float32),
            pltpu.SemaphoreType.DMA((2, var_count // (blocks * BLOCK))),
        ],
        compiler_params=pltpu.CompilerParams(vmem_limit_bytes=VMEM_LIMIT),
        cost_estimate=pl.CostEstimate(
            flops=2 * WINDOW * units * samples * var_count,
            bytes_accessed=4 * (samples + units) * var_count,
            transcendentals=0,
        ),
        name="gene_backward",
    )(lengths, genotypes, delta)


def lane_mask(rows, low):
    lane = lax.broadcasted_iota(jnp.int32, (rows, LANES), 1)
    return lane < LANES // 2 if low else lane >= LANES // 2


def gene_lanes(rows, tiles):
    lane = lax.broadcasted_iota(jnp.int32, (rows, LANES), 1) % tiles
    return [(lane == r).astype(jnp.float32) for r in range(tiles)]


def swap_halves(x):
    half = LANES // 2
    return jnp.concatenate([x[:, half:], x[:, :half]], axis=1)


def fold_kernel(units, which, raw, head, out, wide):
    rows = wide.shape[1]
    start = pl.multiple_of(which[0] * rows, ROWS)
    for c in range(units // 2):
        lanes = slice(c * LANES, (c + 1) * LANES)
        wide[c] = raw[pl.ds(start, rows), lanes].astype(jnp.float32)
    low = lane_mask(SUBLANES, True)

    def body(t, _):
        for c in range(units // 2):
            one = wide[c, pl.ds(t * ROWS, SUBLANES, stride=2), :]
            two = wide[c, pl.ds(t * ROWS + 1, SUBLANES, stride=2), :]
            even = jnp.where(low, one, swap_halves(two))
            odd = jnp.where(low, swap_halves(one), two)
            both = jnp.concatenate([even, odd], axis=0).astype(out.dtype)
            out[pl.ds(pl.multiple_of(t * LANES + c * ROWS, ROWS), ROWS), :] = both
        return 0

    lax.fori_loop(0, rows // ROWS, body, 0, unroll=2)
    out[out.shape[0] - head.shape[0] :, :] = head[...]


def fold_links(raw, head, which, units):
    links, width = raw.shape
    half = links // 2
    rows = half * width // LANES + head.shape[0]
    return pl.pallas_call(
        functools.partial(fold_kernel, units),
        out_shape=jax.ShapeDtypeStruct((rows, LANES), raw.dtype),
        in_specs=[smem, vmem, vmem],
        out_specs=vmem,
        scratch_shapes=[pltpu.VMEM((width // LANES, half, LANES), jnp.float32)],
        compiler_params=pltpu.CompilerParams(vmem_limit_bytes=VMEM_LIMIT),
        cost_estimate=pl.CostEstimate(flops=10**6, bytes_accessed=4 * 10**6, transcendentals=0),
        name="fold_links",
    )(which, raw, head)


def unfold_kernel(units, extra, *refs):
    parts, out, wide = refs[:-2], refs[-2], refs[-1]
    low = lane_mask(SUBLANES, True)
    links = wide.shape[1]

    def body(t, _):
        for c in range(units // 2):
            here = pl.ds(pl.multiple_of(t * LANES + c * ROWS, ROWS), ROWS)
            total = parts[0][here, :].astype(jnp.float32)
            for part in parts[1:]:
                total += part[here, :].astype(jnp.float32)
            even, odd = total[:SUBLANES], total[SUBLANES:]
            one = jnp.where(low, even, swap_halves(odd))
            two = jnp.where(low, swap_halves(even), odd)
            wide[c, pl.ds(t * ROWS, SUBLANES, stride=2), :] = one
            wide[c, pl.ds(t * ROWS + 1, SUBLANES, stride=2), :] = two
        return 0

    lax.fori_loop(0, links // ROWS, body, 0, unroll=2)
    head = sum(part[part.shape[0] - extra :, :].astype(jnp.float32) for part in parts)
    for c in range(units // 2):
        lanes = slice(c * LANES, (c + 1) * LANES)
        out[:links, lanes] = wide[c]
        line = head[c : c + 1] if c < extra // 2 else jnp.zeros((1, LANES), jnp.float32)
        out[links:, lanes] = jnp.broadcast_to(line, (SUBLANES, LANES))


def unfold_sum(parts, units, extra):
    rows = (parts[0].shape[0] - extra) // (units // 2)
    return pl.pallas_call(
        functools.partial(unfold_kernel, units, extra),
        out_shape=jax.ShapeDtypeStruct((rows + SUBLANES, units // 2 * LANES), jnp.float32),
        in_specs=[vmem] * len(parts),
        out_specs=vmem,
        scratch_shapes=[pltpu.VMEM((units // 2, rows, LANES), jnp.float32)],
        compiler_params=pltpu.CompilerParams(vmem_limit_bytes=VMEM_LIMIT),
        cost_estimate=pl.CostEstimate(flops=10**6, bytes_accessed=4 * 10**6, transcendentals=0),
        name="unfold_sum",
    )(*parts)


def link_forward_kernel(half_genes, units, place, members, slots, hidden, *refs):
    weights, outs, sums = refs[: 2 * GROUP], refs[2 * GROUP : -2], refs[-2:]
    quarter, core = place[0], place[1]
    tiles = LANES // units
    for total in sums:
        total[...] = jnp.zeros_like(total)
    keep = [k.astype(jnp.bfloat16) for k in gene_lanes(ROWS, tiles)]
    low = lane_mask(LANES, True).astype(jnp.float32).astype(jnp.bfloat16)
    high = lane_mask(LANES, False).astype(jnp.float32).astype(jnp.bfloat16)
    for piece in range(2 * GROUP):
        source = quarter ^ (piece % GROUP)
        half = core ^ (piece // GROUP)

        def body(t, _, piece=piece, source=source, half=half):
            first = half * half_genes + t * tiles
            at = pl.multiple_of(first * units, LANES)
            own = hidden[source, :, pl.ds(at, LANES)]
            upper, lower = own[:ROWS], own[ROWS:]
            left = jnp.concatenate(
                [jnp.concatenate([upper * k, lower * k], axis=1) for k in keep], axis=0
            )
            block = weights[piece][pl.ds(pl.multiple_of(t * LANES, LANES), LANES), :]
            turned = swap_halves(block)
            right = jnp.concatenate(
                [
                    jnp.concatenate([block * low, turned * low], axis=1),
                    jnp.concatenate([turned * high, block * high], axis=1),
                ],
                axis=0,
            )
            message = nn_dot(left, right)
            gene = source * (2 * half_genes) + first
            for r in range(tiles):
                for m in range(2):
                    slot = slots[members[m, gene + r]]
                    sums[m][slot] += message[
                        r * ROWS : (r + 1) * ROWS, m * LANES : (m + 1) * LANES
                    ]
            return 0

        lax.fori_loop(0, half_genes // tiles, body, 0, unroll=UNROLL)
    shard = outs[0].shape[0]
    for i, out in enumerate(outs):
        out[...] = (
            sums[0][i * shard : (i + 1) * shard] + sums[1][i * shard : (i + 1) * shard]
        ).astype(out.dtype)


def link_forward(place, members, slots, hidden, weights, shards, units):
    half_genes = hidden.shape[2] // units // 2
    slot_count = slots.shape[0]
    out = jax.ShapeDtypeStruct((slot_count // shards, ROWS, LANES), jnp.bfloat16)
    return pl.pallas_call(
        functools.partial(link_forward_kernel, half_genes, units),
        out_shape=[out] * shards,
        in_specs=[smem, smem, smem, vmem] + [vmem] * len(weights),
        out_specs=[vmem] * shards,
        scratch_shapes=[pltpu.VMEM((slot_count, ROWS, LANES), jnp.float32)] * 2,
        compiler_params=pltpu.CompilerParams(vmem_limit_bytes=VMEM_LIMIT),
        cost_estimate=pl.CostEstimate(
            flops=4 * 10**9, bytes_accessed=8 * 10**6, transcendentals=0
        ),
        name="link_forward",
    )(place, members, slots, hidden, *weights)


def link_backward_kernel(half_genes, units, far, place, members, slots, hidden, head, *refs):
    weights, deltas = refs[:GROUP], refs[GROUP : -3 if far else -4]
    out, grads, table = refs[-3:]
    quarter, core = place[0], place[1]
    tiles = LANES // units
    samples = hidden.shape[1]
    shard = deltas[0].shape[0]
    for i, delta in enumerate(deltas):
        table[i * shard : (i + 1) * shard] = delta[...]
    low = lane_mask(ROWS, True).astype(jnp.float32).astype(jnp.bfloat16)
    high = lane_mask(ROWS, False).astype(jnp.float32).astype(jnp.bfloat16)
    keep = gene_lanes(samples, tiles)
    row_gene = lax.broadcasted_iota(jnp.int32, (LANES, LANES), 0) % tiles
    lane_gene = lax.broadcasted_iota(jnp.int32, (LANES, LANES), 1) // samples
    fits = [
        (row_gene == lane_gene + i * (LANES // samples)).astype(jnp.float32)
        for i in range(tiles * samples // LANES)
    ]
    half = core ^ far
    begin = pl.multiple_of(0 if far else half * (half_genes * units), LANES)
    if not far:
        other = pl.multiple_of((1 - half) * (half_genes * units), LANES)
        out[:, :, pl.ds(other, half_genes * units)] = refs[-4][...]
    for piece in range(GROUP):
        source = quarter ^ piece

        def body(t, _, piece=piece, source=source):
            first = half * half_genes + t * tiles
            at = pl.multiple_of(first * units, LANES)
            here = pl.multiple_of(t * LANES, LANES)
            own = hidden[source, :, pl.ds(at, LANES)].astype(jnp.float32)
            gene = source * (2 * half_genes) + first
            parts = []
            for r in range(tiles):
                one = table[slots[members[0, gene + r]]]
                two = table[slots[members[1, gene + r]]]
                parts.append(one * low + swap_halves(two) * high)
                parts.append(swap_halves(one) * low + two * high)
            right = jnp.concatenate(parts, axis=0)
            wide = nt_dot(right, weights[piece][pl.ds(here, LANES), :])
            back = wide[:samples] * keep[0]
            for r in range(1, tiles):
                back += wide[r * samples : (r + 1) * samples] * keep[r]
            back = (back * (1.0 - own * own)).astype(out.dtype)
            out[source, :, pl.ds(pl.multiple_of(begin + here, LANES), LANES)] = back
            flat = jnp.concatenate([own] * (LANES // samples), axis=0).T
            left = jnp.concatenate([(flat * fit).astype(jnp.bfloat16) for fit in fits], axis=1)
            grads[piece, pl.ds(here, LANES), :] = nn_dot(left, right).astype(grads.dtype)
            return 0

        lax.fori_loop(0, half_genes // tiles, body, 0, unroll=UNROLL)
        count = head.shape[0] // (2 * GROUP)
        lines = head[pl.ds(pl.multiple_of((2 * source + half) * count, count), count), :]
        lines = jnp.concatenate([lines, jnp.zeros_like(lines)], axis=0)
        grads[piece, half_genes * units :, :] = lines.astype(grads.dtype)


def link_backward(place, members, slots, hidden, head, weights, deltas, far, units):
    group, samples, width = hidden.shape
    rows = width // 2
    extra = head.shape[0] // GROUP
    grads = jax.ShapeDtypeStruct((GROUP, rows + extra, LANES), jnp.bfloat16)
    outside = far is None
    back = jax.ShapeDtypeStruct((group, samples, rows if outside else width), jnp.bfloat16)
    more = [] if outside else [far]
    operands = [*weights, *deltas, *more]
    return pl.pallas_call(
        functools.partial(link_backward_kernel, rows // units, units, int(outside)),
        out_shape=[back, grads],
        in_specs=[smem, smem, smem] + [vmem] * (2 + len(operands)),
        out_specs=[vmem, vmem],
        scratch_shapes=[pltpu.VMEM((slots.shape[0], ROWS, LANES), jnp.bfloat16)],
        compiler_params=pltpu.CompilerParams(vmem_limit_bytes=VMEM_LIMIT),
        cost_estimate=pl.CostEstimate(
            flops=3 * 10**9, bytes_accessed=20 * 10**6, transcendentals=0
        ),
        name="link_backward",
    )(place, members, slots, hidden, head, *operands)


def on_device(
    genotypes,
    gene_weight,
    gene_lengths,
    membership,
    pathway_slot,
    pathway_weight,
    head_weight,
    cotangent,
):
    devices = lax.axis_size("genes")
    index = lax.axis_index("genes")
    core = lax.axis_index("batch")
    planes = devices // GROUP
    plane, quarter = index // GROUP, index % GROUP
    gene_count = gene_lengths.shape[0]
    units = gene_weight.shape[0]
    path_units = pathway_weight.shape[1] // units
    slot_count = pathway_slot.shape[0]
    shard = slot_count // planes
    samples = genotypes.shape[0]
    part = samples // GROUP
    in_plane = [[GROUP * z + q for q in range(GROUP)] for z in range(planes)]
    along = [[GROUP * z + q for z in range(planes)] for q in range(GROUP)]
    paired = planes == 4

    def swap_plane(x, d):
        pairs = [(GROUP * z + q, GROUP * z + (q ^ d)) for z in range(planes) for q in range(GROUP)]
        return lax.ppermute(x, "genes", pairs)

    def swap_along(x, d):
        pairs = [(GROUP * z + q, GROUP * (z ^ d) + q) for z in range(planes) for q in range(GROUP)]
        return lax.ppermute(x, "genes", pairs)

    def swap_core(x):
        return lax.ppermute(x, "batch", [(0, 1), (1, 0)])

    def spread(x, groups):
        return lax.all_to_all(
            x, "genes", split_axis=0, concat_axis=0, tiled=True, axis_index_groups=groups
        )

    def after(x, *others):
        return lax.optimization_barrier((x, *others))[0]

    with jax.named_scope("link_weights"):
        head_rows = head_weight.reshape(-1, LANES)
        mine = fold_links(pathway_weight, head_rows, core[None].astype(jnp.int32), units)
        near = [mine] + [swap_plane(mine, d) for d in range(1, GROUP)]

    with jax.named_scope("hidden"):
        hidden = gene_forward(genotypes, gene_weight, gene_lengths)
        other_raw, hidden = lax.optimization_barrier((pathway_weight, hidden))
        hidden = spread(hidden.reshape(GROUP, part, gene_count * units), in_plane)

    with jax.named_scope("link_weights"):
        other = fold_links(other_raw, head_rows, (1 - core)[None].astype(jnp.int32), units)
        far = [other] + [swap_core(x) for x in near[1:]]

    with jax.named_scope("tables"):
        place = jnp.stack([quarter, core]).astype(jnp.int32)
        members = lax.dynamic_slice_in_dim(
            membership, plane * GROUP * gene_count, GROUP * gene_count
        ).T
        slots = pathway_slot ^ (plane * shard) if paired else pathway_slot
        heads = jnp.stack([x[-head_rows.shape[0] :] for x in near])
        head = jnp.concatenate(
            [lax.dynamic_slice_in_dim(heads, quarter ^ d, 1) for d in range(GROUP)]
        )
        head = head.reshape(shard, 1, 1, path_units).astype(jnp.float32)
        cot = lax.dynamic_slice_in_dim(cotangent, quarter * part, part)
        cot = cot.reshape(part // ROWS, ROWS).T.reshape(1, ROWS, part // ROWS, 1)

    def head_step(total, head):
        count = total.shape[0]
        active = jnp.tanh(total.reshape(count, ROWS, part // ROWS, path_units))
        delta = (cot * head * (1.0 - active * active)).astype(jnp.bfloat16)
        return jnp.sum(active * cot, axis=(1, 2)), delta.reshape(count, ROWS, LANES)

    if paired:
        cuts = 2
        count = shard // cuts
        with jax.named_scope("pathway_sum"):
            sums = link_forward(
                place, members, slots, hidden, near + far, planes * cuts, units
            )
            passed = [
                sums[2 * cuts + c].astype(jnp.float32)
                + swap_along(sums[3 * cuts + c], 1).astype(jnp.float32)
                for c in range(cuts)
            ]
            passed = [x.astype(jnp.bfloat16) for x in passed]
            crossed = [swap_along(x, 2) for x in passed]
            beside = [swap_along(after(sums[cuts + c], passed[c]), 1) for c in range(cuts)]
        own, heads = [], []
        for c in range(cuts):
            with jax.named_scope("head"):
                across = after(crossed[c], own[-1]) if c else crossed[c]
                total = (
                    sums[c].astype(jnp.float32)
                    + across.astype(jnp.float32)
                    + beside[c].astype(jnp.float32)
                )
                part_sum, delta = head_step(total, head[c * count : (c + 1) * count])
                own.append(delta)
                heads.append(part_sum)
        head_part = jnp.concatenate(heads)
        with jax.named_scope("pathway_delta"):
            two = [swap_along(x, 2) for x in own]
            one = [swap_along(x, 1) for x in own]
            three = [swap_along(x, 1) for x in two]
            deltas = own + one + two + three
    else:
        with jax.named_scope("pathway_sum"):
            sums = link_forward(place, members, slots, hidden, near + far, planes, units)
            parts = spread(jnp.stack(sums), along)
            total = jnp.sum(parts.astype(jnp.float32), axis=0)
        with jax.named_scope("head"):
            head_part, delta = head_step(total, head)
        with jax.named_scope("pathway_delta"):
            every = lax.all_gather(delta, "genes", axis=0, axis_index_groups=along)
            deltas = [every[i] for i in range(planes)]

    with jax.named_scope("link_grads"):
        head_part = head_part.reshape(-1, LANES)
        extra = head_part.shape[0] // GROUP
        back, give = link_backward(
            place, members, slots, hidden, head_part, far, deltas, None, units
        )
        back, give, *deltas = lax.optimization_barrier((back, give, *deltas))
        back, keep = link_backward(
            place, members, slots, hidden, head_part, near, deltas, back, units
        )
        back = spread(back, in_plane).reshape(samples, gene_count * units)

    with jax.named_scope("grad_pathway"):
        given = swap_core(give)
        summed = [
            (keep[d].astype(jnp.float32) + given[d].astype(jnp.float32)).astype(jnp.bfloat16)
            for d in range(GROUP)
        ]
        parts = [summed[0]] + [swap_plane(summed[d], d) for d in range(1, GROUP)]

    with jax.named_scope("grad_gene"):
        rows = gene_backward(genotypes, back, gene_lengths, units)

    with jax.named_scope("grad_pathway"):
        rows, *parts = lax.optimization_barrier((rows, *parts))
        own = unfold_sum(parts, units, extra)
        theirs = swap_core(own)
        links = pathway_weight.shape[0] // 2
        first = jnp.where(core == 0, own, theirs)
        second = jnp.where(core == 0, theirs, own)
        grad_pathway = jnp.concatenate([first[:links], second[:links]], axis=0)
        width = extra // 2 * LANES
        grad_head = jnp.concatenate([first[links, :width], second[links, :width]])

    with jax.named_scope("grad_gene"):
        grad_gene = rows.astype(jnp.float32) + swap_core(rows).astype(jnp.float32)

    return (grad_gene, grad_pathway, grad_head)


def solution(mesh):
    return jax.shard_map(
        on_device,
        mesh=mesh,
        in_specs=(
            P("batch", "genes"),
            P(None, "genes"),
            P("genes"),
            P(),
            P(),
            P("genes", None),
            P("genes"),
            P("batch"),
        ),
        out_specs=(P(None, "genes"), P("genes", None), P("genes")),
        check_vma=False,
    )
```

```python
import functools

import jax
import jax.numpy as jnp
from jax import lax
from jax.experimental import pallas as pl
from jax.experimental.pallas import tpu as pltpu
from jax.sharding import PartitionSpec as P

BLOCK = 512
MIN_GENE = 128
WINDOW = BLOCK // MIN_GENE + 1
GROUP = 4
LANES = 128
ROWS = 16
SUBLANES = 8
UNROLL = 12
MIB = 1024 * 1024

smem = pl.BlockSpec(memory_space=pltpu.SMEM)
vmem = pl.BlockSpec(memory_space=pltpu.VMEM)
hbm = pl.BlockSpec(memory_space=pl.ANY)


def nt_dot(left, right):
    return lax.dot_general(
        left, right, (((1,), (1,)), ((), ())), preferred_element_type=jnp.float32
    )


def nn_dot(left, right):
    return jnp.dot(left, right, preferred_element_type=jnp.float32)


def chunk_blocks(var_count, most):
    total = var_count // BLOCK
    return next(n for n in range(most, 0, -1) if total % n == 0)


def window_edges(lengths, gene_count, gene, start):
    edges = [start]
    for j in range(WINDOW):
        at = gene + j
        length = lengths[jnp.minimum(at, gene_count - 1)]
        edges.append(edges[-1] + jnp.where(at < gene_count, length, 0))
    return edges


def next_window(edges, gene, base):
    start = edges[0]
    for edge in edges[1:]:
        passed = edge <= base
        gene = gene + passed.astype(jnp.int32)
        start = jnp.where(passed, edge, start)
    return gene, start


def reached(edges, base):
    position = lax.broadcasted_iota(jnp.int32, (SUBLANES, BLOCK), 1)
    return [position >= edge - base for edge in edges]


def gene_forward_kernel(
    gene_count, blocks, lengths, geno_hbm, weight_hbm, out, geno, weight, pre, sems
):
    units = weight.shape[0]
    cols = blocks * BLOCK
    chunks = geno.shape[1] // cols

    def copies(c):
        at = pl.ds(pl.multiple_of(c * cols, cols), cols)
        return (
            pltpu.make_async_copy(geno_hbm.at[:, at], geno.at[:, at], sems.at[0, c]),
            pltpu.make_async_copy(weight_hbm.at[:, at], weight.at[:, at], sems.at[1, c]),
        )

    for c in range(chunks):
        for copy in copies(c):
            copy.start()
    pre[...] = jnp.zeros_like(pre)

    def chunk(c, carry):
        gene, start = carry
        for copy in copies(c):
            copy.wait()
        for i in range(blocks):
            base = c * cols + i * BLOCK
            at = pl.ds(pl.multiple_of(base, BLOCK), BLOCK)
            edges = window_edges(lengths, gene_count, gene, start)
            marks = reached(edges, base)
            wide = weight[:, at]
            rows = []
            for j in range(WINDOW):
                mark = (marks[j] & ~marks[j + 1]).astype(jnp.float32)
                mark = jnp.concatenate([mark] * (units // SUBLANES), axis=0)
                rows.append(wide * mark.astype(wide.dtype))
            part = nt_dot(jnp.concatenate(rows, axis=0), geno[:, at])
            where = pl.ds(pl.multiple_of(gene * units, units), WINDOW * units)
            pre[where, :] += part
            gene, start = next_window(edges, gene, base + BLOCK)
        return gene, start

    lax.fori_loop(0, chunks, chunk, (jnp.int32(0), jnp.int32(0)))

    def body(i, _):
        at = pl.multiple_of(i * LANES, LANES)
        tile = jnp.concatenate(
            [pre[pl.ds(at + u, LANES // units, stride=units), :] for u in range(units)], axis=0
        )
        out[:, pl.ds(at, LANES)] = jnp.tanh(tile).T.astype(jnp.bfloat16)
        return 0

    lax.fori_loop(0, gene_count * units // LANES, body, 0, unroll=4)


def gene_forward(genotypes, gene_weight, lengths):
    samples, var_count = genotypes.shape
    units = gene_weight.shape[0]
    gene_count = lengths.shape[0]
    blocks = chunk_blocks(var_count, 16)
    return pl.pallas_call(
        functools.partial(gene_forward_kernel, gene_count, blocks),
        out_shape=jax.ShapeDtypeStruct((samples, gene_count * units), jnp.bfloat16),
        in_specs=[smem, hbm, hbm],
        out_specs=vmem,
        scratch_shapes=[
            pltpu.VMEM(genotypes.shape, jnp.bfloat16),
            pltpu.VMEM(gene_weight.shape, jnp.bfloat16),
            pltpu.VMEM(((gene_count + WINDOW) * units, samples), jnp.float32),
            pltpu.SemaphoreType.DMA((2, var_count // (blocks * BLOCK))),
        ],
        compiler_params=pltpu.CompilerParams(vmem_limit_bytes=52 * MIB),
        cost_estimate=pl.CostEstimate(
            flops=2 * WINDOW * units * samples * var_count,
            bytes_accessed=2 * (samples + units) * var_count,
            transcendentals=gene_count * units * samples,
        ),
        name="gene_forward",
    )(lengths, genotypes, gene_weight)


def gene_backward_kernel(
    gene_count, blocks, lengths, geno_hbm, delta, out_hbm, geno, out, rows, sems
):
    units = out.shape[0]
    cols = blocks * BLOCK
    chunks = geno.shape[1] // cols

    def chunk_copy(c):
        at = pl.ds(pl.multiple_of(c * cols, cols), cols)
        return pltpu.make_async_copy(geno_hbm.at[:, at], geno.at[:, at], sems.at[0, c])

    def chunk_store(c):
        at = pl.ds(pl.multiple_of(c * cols, cols), cols)
        return pltpu.make_async_copy(out.at[:, at], out_hbm.at[:, at], sems.at[1, c])

    for c in range(chunks):
        chunk_copy(c).start()
    tail = WINDOW * units
    rows[gene_count * units :, :] = jnp.zeros((tail, rows.shape[1]), rows.dtype)

    count = LANES // units

    def body(i, _):
        at = pl.multiple_of(i * LANES, LANES)
        tile = delta[:, pl.ds(at, LANES)].astype(jnp.float32).T
        for u in range(units):
            here = pl.ds(at + u, count, stride=units)
            rows[here, :] = tile[u * count : (u + 1) * count]
        return 0

    lax.fori_loop(0, delta.shape[1] // LANES, body, 0, unroll=4)

    def chunk(c, carry):
        gene, start = carry
        chunk_copy(c).wait()
        for i in range(blocks):
            base = c * cols + i * BLOCK
            at = pl.ds(pl.multiple_of(base, BLOCK), BLOCK)
            edges = window_edges(lengths, gene_count, gene, start)
            marks = reached(edges, base)
            where = pl.ds(pl.multiple_of(gene * units, units), WINDOW * units)
            terms = nn_dot(rows[where, :].astype(jnp.bfloat16), geno[:, at])
            pieces = []
            for u in range(0, units, SUBLANES):
                total = terms[u : u + SUBLANES]
                for j in range(1, WINDOW):
                    here = j * units + u
                    total = jnp.where(marks[j], terms[here : here + SUBLANES], total)
                pieces.append(total)
            out[:, at] = jnp.concatenate(pieces, axis=0).astype(out.dtype)
            gene, start = next_window(edges, gene, base + BLOCK)
        chunk_store(c).start()
        return gene, start

    lax.fori_loop(0, chunks, chunk, (jnp.int32(0), jnp.int32(0)))
    for c in range(chunks):
        chunk_store(c).wait()


def gene_backward(genotypes, delta, lengths, units):
    samples, var_count = genotypes.shape
    gene_count = lengths.shape[0]
    blocks = chunk_blocks(var_count, 8)
    return pl.pallas_call(
        functools.partial(gene_backward_kernel, gene_count, blocks),
        out_shape=jax.ShapeDtypeStruct((units, var_count), jnp.bfloat16),
        in_specs=[smem, hbm, vmem],
        out_specs=hbm,
        scratch_shapes=[
            pltpu.VMEM(genotypes.shape, jnp.bfloat16),
            pltpu.VMEM((units, var_count), jnp.bfloat16),
            pltpu.VMEM(((gene_count + WINDOW) * units, samples), jnp.float32),
            pltpu.SemaphoreType.DMA((2, var_count // (blocks * BLOCK))),
        ],
        compiler_params=pltpu.CompilerParams(vmem_limit_bytes=52 * MIB),
        cost_estimate=pl.CostEstimate(
            flops=2 * WINDOW * units * samples * var_count,
            bytes_accessed=4 * (samples + units) * var_count,
            transcendentals=0,
        ),
        name="gene_backward",
    )(lengths, genotypes, delta)


def lane_mask(rows, low):
    lane = lax.broadcasted_iota(jnp.int32, (rows, LANES), 1)
    return lane < LANES // 2 if low else lane >= LANES // 2


def gene_lanes(rows, tiles):
    lane = lax.broadcasted_iota(jnp.int32, (rows, LANES), 1) % tiles
    return [(lane == r).astype(jnp.float32) for r in range(tiles)]


def swap_halves(x):
    half = LANES // 2
    return jnp.concatenate([x[:, half:], x[:, :half]], axis=1)


def fold_kernel(units, which, raw, head, out, wide):
    rows = wide.shape[1]
    start = pl.multiple_of(which[0] * rows, ROWS)
    for c in range(units // 2):
        lanes = slice(c * LANES, (c + 1) * LANES)
        wide[c] = raw[pl.ds(start, rows), lanes].astype(jnp.float32)
    low = lane_mask(SUBLANES, True)

    def body(t, _):
        for c in range(units // 2):
            one = wide[c, pl.ds(t * ROWS, SUBLANES, stride=2), :]
            two = wide[c, pl.ds(t * ROWS + 1, SUBLANES, stride=2), :]
            even = jnp.where(low, one, swap_halves(two))
            odd = jnp.where(low, swap_halves(one), two)
            both = jnp.concatenate([even, odd], axis=0).astype(out.dtype)
            out[pl.ds(pl.multiple_of(t * LANES + c * ROWS, ROWS), ROWS), :] = both
        return 0

    lax.fori_loop(0, rows // ROWS, body, 0, unroll=2)
    out[out.shape[0] - head.shape[0] :, :] = head[...]


def fold_links(raw, head, which, units):
    links, width = raw.shape
    half = links // 2
    rows = half * width // LANES + head.shape[0]
    return pl.pallas_call(
        functools.partial(fold_kernel, units),
        out_shape=jax.ShapeDtypeStruct((rows, LANES), raw.dtype),
        in_specs=[smem, vmem, vmem],
        out_specs=vmem,
        scratch_shapes=[pltpu.VMEM((width // LANES, half, LANES), jnp.float32)],
        compiler_params=pltpu.CompilerParams(vmem_limit_bytes=8 * MIB),
        cost_estimate=pl.CostEstimate(flops=10**6, bytes_accessed=4 * 10**6, transcendentals=0),
        name="fold_links",
    )(which, raw, head)


def unfold_kernel(units, extra, *refs):
    parts, out, wide = refs[:-2], refs[-2], refs[-1]
    low = lane_mask(SUBLANES, True)
    links = wide.shape[1]

    def body(t, _):
        for c in range(units // 2):
            here = pl.ds(pl.multiple_of(t * LANES + c * ROWS, ROWS), ROWS)
            total = parts[0][here, :].astype(jnp.float32)
            for part in parts[1:]:
                total += part[here, :].astype(jnp.float32)
            even, odd = total[:SUBLANES], total[SUBLANES:]
            one = jnp.where(low, even, swap_halves(odd))
            two = jnp.where(low, swap_halves(even), odd)
            wide[c, pl.ds(t * ROWS, SUBLANES, stride=2), :] = one
            wide[c, pl.ds(t * ROWS + 1, SUBLANES, stride=2), :] = two
        return 0

    lax.fori_loop(0, links // ROWS, body, 0, unroll=2)
    head = sum(part[part.shape[0] - extra :, :].astype(jnp.float32) for part in parts)
    head = head[: extra // 2] + head[extra // 2 :]
    for c in range(units // 2):
        lanes = slice(c * LANES, (c + 1) * LANES)
        out[:links, lanes] = wide[c]
        line = head[c : c + 1] if c < extra // 2 else jnp.zeros((1, LANES), jnp.float32)
        out[links:, lanes] = jnp.broadcast_to(line, (SUBLANES, LANES))


def unfold_sum(parts, units, extra):
    rows = (parts[0].shape[0] - extra) // (units // 2)
    return pl.pallas_call(
        functools.partial(unfold_kernel, units, extra),
        out_shape=jax.ShapeDtypeStruct((rows + SUBLANES, units // 2 * LANES), jnp.float32),
        in_specs=[vmem] * len(parts),
        out_specs=vmem,
        scratch_shapes=[pltpu.VMEM((units // 2, rows, LANES), jnp.float32)],
        compiler_params=pltpu.CompilerParams(vmem_limit_bytes=10 * MIB),
        cost_estimate=pl.CostEstimate(flops=10**6, bytes_accessed=4 * 10**6, transcendentals=0),
        name="unfold_sum",
    )(*parts)


def link_forward_kernel(half_genes, units, place, members, slots, hidden, *refs):
    weights, outs, sums = refs[: 2 * GROUP], refs[2 * GROUP : -2], refs[-2:]
    quarter, core = place[0], place[1]
    tiles = LANES // units
    for total in sums:
        total[...] = jnp.zeros_like(total)
    keep = [k.astype(jnp.bfloat16) for k in gene_lanes(ROWS, tiles)]
    low = lane_mask(LANES, True).astype(jnp.float32).astype(jnp.bfloat16)
    high = lane_mask(LANES, False).astype(jnp.float32).astype(jnp.bfloat16)
    for piece in range(2 * GROUP):
        source = quarter ^ (piece % GROUP)
        half = core ^ (piece // GROUP)

        def body(t, _, piece=piece, source=source, half=half):
            first = half * half_genes + t * tiles
            at = pl.multiple_of(first * units, LANES)
            own = hidden[source, :, pl.ds(at, LANES)]
            upper, lower = own[:ROWS], own[ROWS:]
            left = jnp.concatenate(
                [jnp.concatenate([upper * k, lower * k], axis=1) for k in keep], axis=0
            )
            block = weights[piece][pl.ds(pl.multiple_of(t * LANES, LANES), LANES), :]
            turned = swap_halves(block)
            right = jnp.concatenate(
                [
                    jnp.concatenate([block * low, turned * low], axis=1),
                    jnp.concatenate([turned * high, block * high], axis=1),
                ],
                axis=0,
            )
            message = nn_dot(left, right)
            gene = source * (2 * half_genes) + first
            for r in range(tiles):
                for m in range(2):
                    slot = slots[members[m, gene + r]]
                    sums[m][slot] += message[
                        r * ROWS : (r + 1) * ROWS, m * LANES : (m + 1) * LANES
                    ]
            return 0

        lax.fori_loop(0, half_genes // tiles, body, 0, unroll=UNROLL)
    shard = outs[0].shape[0]
    for i, out in enumerate(outs):
        out[...] = (
            sums[0][i * shard : (i + 1) * shard] + sums[1][i * shard : (i + 1) * shard]
        ).astype(out.dtype)


def link_forward(place, members, slots, hidden, weights, shards, units):
    half_genes = hidden.shape[2] // units // 2
    slot_count = slots.shape[0]
    out = jax.ShapeDtypeStruct((slot_count // shards, ROWS, LANES), jnp.bfloat16)
    return pl.pallas_call(
        functools.partial(link_forward_kernel, half_genes, units),
        out_shape=[out] * shards,
        in_specs=[smem, smem, smem, vmem] + [vmem] * len(weights),
        out_specs=[vmem] * shards,
        scratch_shapes=[pltpu.VMEM((slot_count, ROWS, LANES), jnp.float32)] * 2,
        compiler_params=pltpu.CompilerParams(vmem_limit_bytes=slot_count * ROWS * LANES * 10 + 8 * MIB),
        cost_estimate=pl.CostEstimate(
            flops=4 * 10**9, bytes_accessed=8 * 10**6, transcendentals=0
        ),
        name="link_forward",
    )(place, members, slots, hidden, *weights)


def link_backward_kernel(half_genes, units, place, members, slots, hidden, head, *refs):
    weights, deltas = refs[: 2 * GROUP], refs[2 * GROUP : -4]
    out, keeps, gives, table = refs[-4:]
    quarter, core = place[0], place[1]
    tiles = LANES // units
    samples = hidden.shape[1]
    shard = deltas[0].shape[0]
    for i, delta in enumerate(deltas):
        table[i * shard : (i + 1) * shard] = delta[...]
    low = lane_mask(ROWS, True).astype(jnp.float32).astype(jnp.bfloat16)
    high = lane_mask(ROWS, False).astype(jnp.float32).astype(jnp.bfloat16)
    keep = gene_lanes(samples, tiles)
    row_gene = lax.broadcasted_iota(jnp.int32, (LANES, LANES), 0) % tiles
    lane_gene = lax.broadcasted_iota(jnp.int32, (LANES, LANES), 1) // samples
    fits = [
        (row_gene == lane_gene + i * (LANES // samples)).astype(jnp.float32)
        for i in range(tiles * samples // LANES)
    ]
    for index in range(2 * GROUP):
        piece = index % GROUP
        grads = gives if index // GROUP else keeps
        source = quarter ^ piece
        half = core ^ (index // GROUP)

        def body(t, _, index=index, piece=piece, grads=grads, source=source, half=half):
            first = half * half_genes + t * tiles
            at = pl.multiple_of(first * units, LANES)
            here = pl.multiple_of(t * LANES, LANES)
            own = hidden[source, :, pl.ds(at, LANES)].astype(jnp.float32)
            gene = source * (2 * half_genes) + first
            parts = []
            for r in range(tiles):
                one = table[slots[members[0, gene + r]]]
                two = table[slots[members[1, gene + r]]]
                parts.append(one * low + swap_halves(two) * high)
                parts.append(swap_halves(one) * low + two * high)
            right = jnp.concatenate(parts, axis=0)
            wide = nt_dot(right, weights[index][pl.ds(here, LANES), :])
            back = wide[:samples] * keep[0]
            for r in range(1, tiles):
                back += wide[r * samples : (r + 1) * samples] * keep[r]
            out[source, :, pl.ds(at, LANES)] = (back * (1.0 - own * own)).astype(out.dtype)
            flat = jnp.concatenate([own] * (LANES // samples), axis=0).T
            left = jnp.concatenate([(flat * fit).astype(jnp.bfloat16) for fit in fits], axis=1)
            grads[piece, pl.ds(here, LANES), :] = nn_dot(left, right).astype(grads.dtype)
            return 0

        lax.fori_loop(0, half_genes // tiles, body, 0, unroll=UNROLL)
        count = head.shape[0] // (2 * GROUP)
        lines = head[pl.ds(pl.multiple_of((2 * source + half) * count, count), count), :]
        coarse = lines.astype(grads.dtype).astype(jnp.float32)
        lines = jnp.concatenate([coarse, lines - coarse], axis=0)
        grads[piece, half_genes * units :, :] = lines.astype(grads.dtype)


def link_backward(place, members, slots, hidden, head, weights, deltas, units):
    rows = hidden.shape[2] // 2
    extra = head.shape[0] // GROUP
    grads = jax.ShapeDtypeStruct((GROUP, rows + extra, LANES), jnp.bfloat16)
    operands = [*weights, *deltas]
    return pl.pallas_call(
        functools.partial(link_backward_kernel, rows // units, units),
        out_shape=[jax.ShapeDtypeStruct(hidden.shape, jnp.bfloat16), grads, grads],
        in_specs=[smem, smem, smem] + [vmem] * (2 + len(operands)),
        out_specs=[vmem] * 3,
        scratch_shapes=[pltpu.VMEM((slots.shape[0], ROWS, LANES), jnp.bfloat16)],
        compiler_params=pltpu.CompilerParams(vmem_limit_bytes=56 * MIB),
        cost_estimate=pl.CostEstimate(
            flops=6 * 10**9, bytes_accessed=20 * 10**6, transcendentals=0
        ),
        name="link_backward",
    )(place, members, slots, hidden, head, *operands)


def on_device(
    genotypes,
    gene_weight,
    gene_lengths,
    membership,
    pathway_slot,
    pathway_weight,
    head_weight,
    cotangent,
):
    devices = lax.axis_size("genes")
    index = lax.axis_index("genes")
    core = lax.axis_index("batch")
    planes = devices // GROUP
    plane, quarter = index // GROUP, index % GROUP
    gene_count = gene_lengths.shape[0]
    units = gene_weight.shape[0]
    path_units = pathway_weight.shape[1] // units
    slot_count = pathway_slot.shape[0]
    shard = slot_count // planes
    samples = genotypes.shape[0]
    part = samples // GROUP
    in_plane = [[GROUP * z + q for q in range(GROUP)] for z in range(planes)]
    along = [[GROUP * z + q for z in range(planes)] for q in range(GROUP)]
    paired = planes == 4

    def swap_plane(x, d):
        pairs = [(GROUP * z + q, GROUP * z + (q ^ d)) for z in range(planes) for q in range(GROUP)]
        return lax.ppermute(x, "genes", pairs)

    def swap_along(x, d):
        pairs = [(GROUP * z + q, GROUP * (z ^ d) + q) for z in range(planes) for q in range(GROUP)]
        return lax.ppermute(x, "genes", pairs)

    def swap_core(x):
        return lax.ppermute(x, "batch", [(0, 1), (1, 0)])

    def spread(x, groups):
        return lax.all_to_all(
            x, "genes", split_axis=0, concat_axis=0, tiled=True, axis_index_groups=groups
        )

    def after(x, *others):
        return lax.optimization_barrier((x, *others))[0]

    with jax.named_scope("link_weights"):
        head_rows = head_weight.reshape(-1, LANES)
        mine = fold_links(pathway_weight, head_rows, core[None].astype(jnp.int32), units)
        near = [mine] + [swap_plane(mine, d) for d in range(1, GROUP)]

    with jax.named_scope("hidden"):
        hidden = gene_forward(genotypes, gene_weight, gene_lengths)
        other_raw, hidden = lax.optimization_barrier((pathway_weight, hidden))
        hidden = spread(hidden.reshape(GROUP, part, gene_count * units), in_plane)

    with jax.named_scope("link_weights"):
        other = fold_links(other_raw, head_rows, (1 - core)[None].astype(jnp.int32), units)
        far = [other] + [swap_core(x) for x in near[1:]]

    with jax.named_scope("tables"):
        place = jnp.stack([quarter, core]).astype(jnp.int32)
        members = lax.dynamic_slice_in_dim(
            membership, plane * GROUP * gene_count, GROUP * gene_count
        ).T
        slots = pathway_slot ^ (plane * shard) if paired else pathway_slot
        heads = jnp.stack([x[-head_rows.shape[0] :] for x in near])
        head = jnp.concatenate(
            [lax.dynamic_slice_in_dim(heads, quarter ^ d, 1) for d in range(GROUP)]
        )
        head = head.reshape(shard, 1, 1, path_units).astype(jnp.float32)
        cot = lax.dynamic_slice_in_dim(cotangent, quarter * part, part)
        cot = cot.reshape(part // ROWS, ROWS).T.reshape(1, ROWS, part // ROWS, 1)

    def head_step(total, head):
        count = total.shape[0]
        active = jnp.tanh(total.reshape(count, ROWS, part // ROWS, path_units))
        delta = (cot * head * (1.0 - active * active)).astype(jnp.bfloat16)
        return jnp.sum(active * cot, axis=(1, 2)), delta.reshape(count, ROWS, LANES)

    if paired:
        cuts = 2
        count = shard // cuts
        with jax.named_scope("pathway_sum"):
            sums = link_forward(
                place, members, slots, hidden, near + far, planes * cuts, units
            )
            passed = [
                sums[2 * cuts + c].astype(jnp.float32)
                + swap_along(sums[3 * cuts + c], 1).astype(jnp.float32)
                for c in range(cuts)
            ]
            passed = [x.astype(jnp.bfloat16) for x in passed]
            crossed = [swap_along(x, 2) for x in passed]
            beside = [swap_along(after(sums[cuts + c], passed[c]), 1) for c in range(cuts)]
        own, heads = [], []
        for c in range(cuts):
            with jax.named_scope("head"):
                across = after(crossed[c], own[-1]) if c else crossed[c]
                total = (
                    sums[c].astype(jnp.float32)
                    + across.astype(jnp.float32)
                    + beside[c].astype(jnp.float32)
                )
                part_sum, delta = head_step(total, head[c * count : (c + 1) * count])
                own.append(delta)
                heads.append(part_sum)
        head_part = jnp.concatenate(heads)
        with jax.named_scope("pathway_delta"):
            two = [swap_along(x, 2) for x in own]
            one = [swap_along(x, 1) for x in own]
            three = [swap_along(x, 1) for x in two]
            deltas = own + one + two + three
    else:
        with jax.named_scope("pathway_sum"):
            sums = link_forward(place, members, slots, hidden, near + far, planes, units)
            parts = spread(jnp.stack(sums), along)
            total = jnp.sum(parts.astype(jnp.float32), axis=0)
        with jax.named_scope("head"):
            head_part, delta = head_step(total, head)
        with jax.named_scope("pathway_delta"):
            every = lax.all_gather(delta, "genes", axis=0, axis_index_groups=along)
            deltas = [every[i] for i in range(planes)]

    with jax.named_scope("link_grads"):
        head_part = head_part.reshape(-1, LANES)
        extra = head_part.shape[0] // GROUP
        back, keep, give = link_backward(
            place, members, slots, hidden, head_part, near + far, deltas, units
        )
        back = spread(back, in_plane).reshape(samples, gene_count * units)

    with jax.named_scope("grad_pathway"):
        given = swap_core(give)
        summed = [
            (keep[d].astype(jnp.float32) + given[d].astype(jnp.float32)).astype(jnp.bfloat16)
            for d in range(GROUP)
        ]
        parts = [summed[0]] + [swap_plane(summed[d], d) for d in range(1, GROUP)]

    with jax.named_scope("grad_gene"):
        rows = gene_backward(genotypes, back, gene_lengths, units)

    with jax.named_scope("grad_pathway"):
        rows, *parts = lax.optimization_barrier((rows, *parts))
        own = unfold_sum(parts, units, extra)
        grad_gene = rows.astype(jnp.float32) + swap_core(rows).astype(jnp.float32)
        theirs, grad_gene = lax.optimization_barrier((swap_core(own), grad_gene))
        links = pathway_weight.shape[0] // 2
        first = jnp.where(core == 0, own, theirs)
        second = jnp.where(core == 0, theirs, own)
        grad_pathway = jnp.concatenate([first[:links], second[:links]], axis=0)
        width = extra // 2 * LANES
        grad_head = jnp.concatenate([first[links, :width], second[links, :width]])

    return (grad_gene, grad_pathway, grad_head)


def solution(mesh):
    return jax.shard_map(
        on_device,
        mesh=mesh,
        in_specs=(
            P("batch", "genes"),
            P(None, "genes"),
            P("genes"),
            P(),
            P(),
            P("genes", None),
            P("genes"),
            P("batch"),
        ),
        out_specs=(P(None, "genes"), P("genes", None), P("genes")),
        check_vma=False,
    )
```

```python
import functools

import jax
import jax.numpy as jnp
from jax import lax
from jax.experimental import pallas as pl
from jax.experimental.pallas import tpu as pltpu
from jax.sharding import PartitionSpec as P

BLOCK = 512
MIN_GENE = 128
WINDOW = BLOCK // MIN_GENE + 1
GROUP = 4
LANES = 128
ROWS = 16
SUBLANES = 8
UNROLL = 12
MIB = 1024 * 1024

smem = pl.BlockSpec(memory_space=pltpu.SMEM)
vmem = pl.BlockSpec(memory_space=pltpu.VMEM)
hbm = pl.BlockSpec(memory_space=pl.ANY)


def nt_dot(left, right):
    return lax.dot_general(
        left, right, (((1,), (1,)), ((), ())), preferred_element_type=jnp.float32
    )


def nn_dot(left, right):
    return jnp.dot(left, right, preferred_element_type=jnp.float32)


def chunk_blocks(var_count, most):
    total = var_count // BLOCK
    return next(n for n in range(most, 0, -1) if total % n == 0)


def window_edges(lengths, gene_count, gene, start):
    edges = [start]
    for j in range(WINDOW):
        at = gene + j
        length = lengths[jnp.minimum(at, gene_count - 1)]
        edges.append(edges[-1] + jnp.where(at < gene_count, length, 0))
    return edges


def next_window(edges, gene, base):
    start = edges[0]
    for edge in edges[1:]:
        passed = edge <= base
        gene = gene + passed.astype(jnp.int32)
        start = jnp.where(passed, edge, start)
    return gene, start


def reached(edges, base):
    position = lax.broadcasted_iota(jnp.int32, (SUBLANES, BLOCK), 1)
    return [position >= edge - base for edge in edges]


def gene_forward_kernel(
    gene_count, blocks, lengths, geno_hbm, weight_hbm, out, geno, weight, pre, sems
):
    units = weight.shape[0]
    cols = blocks * BLOCK
    chunks = geno.shape[1] // cols

    def copies(c):
        at = pl.ds(pl.multiple_of(c * cols, cols), cols)
        return (
            pltpu.make_async_copy(geno_hbm.at[:, at], geno.at[:, at], sems.at[0, c]),
            pltpu.make_async_copy(weight_hbm.at[:, at], weight.at[:, at], sems.at[1, c]),
        )

    for c in range(chunks):
        for copy in copies(c):
            copy.start()
    pre[...] = jnp.zeros_like(pre)

    def chunk(c, carry):
        gene, start = carry
        for copy in copies(c):
            copy.wait()
        for i in range(blocks):
            base = c * cols + i * BLOCK
            at = pl.ds(pl.multiple_of(base, BLOCK), BLOCK)
            edges = window_edges(lengths, gene_count, gene, start)
            marks = reached(edges, base)
            wide = weight[:, at]
            rows = []
            for j in range(WINDOW):
                mark = (marks[j] & ~marks[j + 1]).astype(jnp.float32)
                mark = jnp.concatenate([mark] * (units // SUBLANES), axis=0)
                rows.append(wide * mark.astype(wide.dtype))
            part = nt_dot(jnp.concatenate(rows, axis=0), geno[:, at])
            where = pl.ds(pl.multiple_of(gene * units, units), WINDOW * units)
            pre[where, :] += part
            gene, start = next_window(edges, gene, base + BLOCK)
        return gene, start

    lax.fori_loop(0, chunks, chunk, (jnp.int32(0), jnp.int32(0)))

    def body(i, _):
        at = pl.multiple_of(i * LANES, LANES)
        tile = jnp.concatenate(
            [pre[pl.ds(at + u, LANES // units, stride=units), :] for u in range(units)], axis=0
        )
        out[:, pl.ds(at, LANES)] = jnp.tanh(tile).T.astype(jnp.bfloat16)
        return 0

    lax.fori_loop(0, gene_count * units // LANES, body, 0, unroll=4)


def gene_forward(genotypes, gene_weight, lengths):
    samples, var_count = genotypes.shape
    units = gene_weight.shape[0]
    gene_count = lengths.shape[0]
    blocks = chunk_blocks(var_count, 16)
    return pl.pallas_call(
        functools.partial(gene_forward_kernel, gene_count, blocks),
        out_shape=jax.ShapeDtypeStruct((samples, gene_count * units), jnp.bfloat16),
        in_specs=[smem, hbm, hbm],
        out_specs=vmem,
        scratch_shapes=[
            pltpu.VMEM(genotypes.shape, jnp.bfloat16),
            pltpu.VMEM(gene_weight.shape, jnp.bfloat16),
            pltpu.VMEM(((gene_count + WINDOW) * units, samples), jnp.float32),
            pltpu.SemaphoreType.DMA((2, var_count // (blocks * BLOCK))),
        ],
        compiler_params=pltpu.CompilerParams(vmem_limit_bytes=52 * MIB),
        cost_estimate=pl.CostEstimate(
            flops=2 * WINDOW * units * samples * var_count,
            bytes_accessed=2 * (samples + units) * var_count,
            transcendentals=gene_count * units * samples,
        ),
        name="gene_forward",
    )(lengths, genotypes, gene_weight)


def gene_backward_kernel(
    gene_count, blocks, lengths, geno_hbm, delta, out_hbm, geno, out, rows, sems
):
    units = out.shape[0]
    cols = blocks * BLOCK
    chunks = geno.shape[1] // cols

    def chunk_copy(c):
        at = pl.ds(pl.multiple_of(c * cols, cols), cols)
        return pltpu.make_async_copy(geno_hbm.at[:, at], geno.at[:, at], sems.at[0, c])

    def chunk_store(c):
        at = pl.ds(pl.multiple_of(c * cols, cols), cols)
        return pltpu.make_async_copy(out.at[:, at], out_hbm.at[:, at], sems.at[1, c])

    for c in range(chunks):
        chunk_copy(c).start()
    tail = WINDOW * units
    rows[gene_count * units :, :] = jnp.zeros((tail, rows.shape[1]), rows.dtype)

    count = LANES // units

    def body(i, _):
        at = pl.multiple_of(i * LANES, LANES)
        tile = delta[:, pl.ds(at, LANES)].astype(jnp.float32).T
        for u in range(units):
            here = pl.ds(at + u, count, stride=units)
            rows[here, :] = tile[u * count : (u + 1) * count]
        return 0

    lax.fori_loop(0, delta.shape[1] // LANES, body, 0, unroll=4)

    def chunk(c, carry):
        gene, start = carry
        chunk_copy(c).wait()
        for i in range(blocks):
            base = c * cols + i * BLOCK
            at = pl.ds(pl.multiple_of(base, BLOCK), BLOCK)
            edges = window_edges(lengths, gene_count, gene, start)
            marks = reached(edges, base)
            where = pl.ds(pl.multiple_of(gene * units, units), WINDOW * units)
            terms = nn_dot(rows[where, :].astype(jnp.bfloat16), geno[:, at])
            pieces = []
            for u in range(0, units, SUBLANES):
                total = terms[u : u + SUBLANES]
                for j in range(1, WINDOW):
                    here = j * units + u
                    total = jnp.where(marks[j], terms[here : here + SUBLANES], total)
                pieces.append(total)
            out[:, at] = jnp.concatenate(pieces, axis=0).astype(out.dtype)
            gene, start = next_window(edges, gene, base + BLOCK)
        chunk_store(c).start()
        return gene, start

    lax.fori_loop(0, chunks, chunk, (jnp.int32(0), jnp.int32(0)))
    for c in range(chunks):
        chunk_store(c).wait()


def gene_backward(genotypes, delta, lengths, units):
    samples, var_count = genotypes.shape
    gene_count = lengths.shape[0]
    blocks = chunk_blocks(var_count, 8)
    return pl.pallas_call(
        functools.partial(gene_backward_kernel, gene_count, blocks),
        out_shape=jax.ShapeDtypeStruct((units, var_count), jnp.bfloat16),
        in_specs=[smem, hbm, vmem],
        out_specs=hbm,
        scratch_shapes=[
            pltpu.VMEM(genotypes.shape, jnp.bfloat16),
            pltpu.VMEM((units, var_count), jnp.bfloat16),
            pltpu.VMEM(((gene_count + WINDOW) * units, samples), jnp.float32),
            pltpu.SemaphoreType.DMA((2, var_count // (blocks * BLOCK))),
        ],
        compiler_params=pltpu.CompilerParams(vmem_limit_bytes=52 * MIB),
        cost_estimate=pl.CostEstimate(
            flops=2 * WINDOW * units * samples * var_count,
            bytes_accessed=4 * (samples + units) * var_count,
            transcendentals=0,
        ),
        name="gene_backward",
    )(lengths, genotypes, delta)


def lane_mask(rows, low):
    lane = lax.broadcasted_iota(jnp.int32, (rows, LANES), 1)
    return lane < LANES // 2 if low else lane >= LANES // 2


def gene_lanes(rows, tiles):
    lane = lax.broadcasted_iota(jnp.int32, (rows, LANES), 1) % tiles
    return [(lane == r).astype(jnp.float32) for r in range(tiles)]


def swap_halves(x):
    half = LANES // 2
    return jnp.concatenate([x[:, half:], x[:, :half]], axis=1)


def fold_kernel(units, which, raw, head, out, wide):
    rows = wide.shape[1]
    start = pl.multiple_of(which[0] * rows, ROWS)
    for c in range(units // 2):
        lanes = slice(c * LANES, (c + 1) * LANES)
        wide[c] = raw[pl.ds(start, rows), lanes].astype(jnp.float32)
    low = lane_mask(SUBLANES, True)

    def body(t, _):
        for c in range(units // 2):
            one = wide[c, pl.ds(t * ROWS, SUBLANES, stride=2), :]
            two = wide[c, pl.ds(t * ROWS + 1, SUBLANES, stride=2), :]
            even = jnp.where(low, one, swap_halves(two))
            odd = jnp.where(low, swap_halves(one), two)
            both = jnp.concatenate([even, odd], axis=0).astype(out.dtype)
            out[pl.ds(pl.multiple_of(t * LANES + c * ROWS, ROWS), ROWS), :] = both
        return 0

    lax.fori_loop(0, rows // ROWS, body, 0, unroll=2)
    out[out.shape[0] - head.shape[0] :, :] = head[...]


def fold_links(raw, head, which, units):
    links, width = raw.shape
    half = links // 2
    rows = half * width // LANES + head.shape[0]
    return pl.pallas_call(
        functools.partial(fold_kernel, units),
        out_shape=jax.ShapeDtypeStruct((rows, LANES), raw.dtype),
        in_specs=[smem, vmem, vmem],
        out_specs=vmem,
        scratch_shapes=[pltpu.VMEM((width // LANES, half, LANES), jnp.float32)],
        compiler_params=pltpu.CompilerParams(vmem_limit_bytes=8 * MIB),
        cost_estimate=pl.CostEstimate(flops=10**6, bytes_accessed=4 * 10**6, transcendentals=0),
        name="fold_links",
    )(which, raw, head)


def unfold_kernel(units, extra, *refs):
    parts, out, wide = refs[:-2], refs[-2], refs[-1]
    low = lane_mask(SUBLANES, True)
    links = wide.shape[1]

    def body(t, _):
        for c in range(units // 2):
            here = pl.ds(pl.multiple_of(t * LANES + c * ROWS, ROWS), ROWS)
            total = parts[0][here, :].astype(jnp.float32)
            for part in parts[1:]:
                total += part[here, :].astype(jnp.float32)
            even, odd = total[:SUBLANES], total[SUBLANES:]
            one = jnp.where(low, even, swap_halves(odd))
            two = jnp.where(low, swap_halves(even), odd)
            wide[c, pl.ds(t * ROWS, SUBLANES, stride=2), :] = one
            wide[c, pl.ds(t * ROWS + 1, SUBLANES, stride=2), :] = two
        return 0

    lax.fori_loop(0, links // ROWS, body, 0, unroll=2)
    head = sum(part[part.shape[0] - extra :, :].astype(jnp.float32) for part in parts)
    head = head[: extra // 2] + head[extra // 2 :]
    for c in range(units // 2):
        lanes = slice(c * LANES, (c + 1) * LANES)
        out[:links, lanes] = wide[c]
        line = head[c : c + 1] if c < extra // 2 else jnp.zeros((1, LANES), jnp.float32)
        out[links:, lanes] = jnp.broadcast_to(line, (SUBLANES, LANES))


def unfold_sum(parts, units, extra):
    rows = (parts[0].shape[0] - extra) // (units // 2)
    return pl.pallas_call(
        functools.partial(unfold_kernel, units, extra),
        out_shape=jax.ShapeDtypeStruct((rows + SUBLANES, units // 2 * LANES), jnp.float32),
        in_specs=[vmem] * len(parts),
        out_specs=vmem,
        scratch_shapes=[pltpu.VMEM((units // 2, rows, LANES), jnp.float32)],
        compiler_params=pltpu.CompilerParams(vmem_limit_bytes=10 * MIB),
        cost_estimate=pl.CostEstimate(flops=10**6, bytes_accessed=4 * 10**6, transcendentals=0),
        name="unfold_sum",
    )(*parts)


def link_forward_kernel(half_genes, units, place, members, slots, hidden, *refs):
    weights, outs, sums = refs[: 2 * GROUP], refs[2 * GROUP : -2], refs[-2:]
    quarter, core = place[0], place[1]
    tiles = LANES // units
    for total in sums:
        total[...] = jnp.zeros_like(total)
    keep = [k.astype(jnp.bfloat16) for k in gene_lanes(ROWS, tiles)]
    low = lane_mask(LANES, True).astype(jnp.float32).astype(jnp.bfloat16)
    high = lane_mask(LANES, False).astype(jnp.float32).astype(jnp.bfloat16)
    for piece in range(2 * GROUP):
        source = quarter ^ (piece % GROUP)
        half = core ^ (piece // GROUP)

        def body(t, _, piece=piece, source=source, half=half):
            first = half * half_genes + t * tiles
            at = pl.multiple_of(first * units, LANES)
            own = hidden[source, :, pl.ds(at, LANES)]
            upper, lower = own[:ROWS], own[ROWS:]
            left = jnp.concatenate(
                [jnp.concatenate([upper * k, lower * k], axis=1) for k in keep], axis=0
            )
            block = weights[piece][pl.ds(pl.multiple_of(t * LANES, LANES), LANES), :]
            turned = swap_halves(block)
            right = jnp.concatenate(
                [
                    jnp.concatenate([block * low, turned * low], axis=1),
                    jnp.concatenate([turned * high, block * high], axis=1),
                ],
                axis=0,
            )
            message = nn_dot(left, right)
            gene = source * (2 * half_genes) + first
            for r in range(tiles):
                for m in range(2):
                    slot = slots[members[m, gene + r]]
                    sums[m][slot] += message[
                        r * ROWS : (r + 1) * ROWS, m * LANES : (m + 1) * LANES
                    ]
            return 0

        lax.fori_loop(0, half_genes // tiles, body, 0, unroll=UNROLL)
    shard = outs[0].shape[0]
    for i, out in enumerate(outs):
        out[...] = (
            sums[0][i * shard : (i + 1) * shard] + sums[1][i * shard : (i + 1) * shard]
        ).astype(out.dtype)


def link_forward(place, members, slots, hidden, weights, shards, units):
    half_genes = hidden.shape[2] // units // 2
    slot_count = slots.shape[0]
    out = jax.ShapeDtypeStruct((slot_count // shards, ROWS, LANES), jnp.bfloat16)
    return pl.pallas_call(
        functools.partial(link_forward_kernel, half_genes, units),
        out_shape=[out] * shards,
        in_specs=[smem, smem, smem, vmem] + [vmem] * len(weights),
        out_specs=[vmem] * shards,
        scratch_shapes=[pltpu.VMEM((slot_count, ROWS, LANES), jnp.float32)] * 2,
        compiler_params=pltpu.CompilerParams(vmem_limit_bytes=slot_count * ROWS * LANES * 10 + 8 * MIB),
        cost_estimate=pl.CostEstimate(
            flops=4 * 10**9, bytes_accessed=8 * 10**6, transcendentals=0
        ),
        name="link_forward",
    )(place, members, slots, hidden, *weights)


def link_backward_kernel(half_genes, units, place, members, slots, hidden, head, *refs):
    weights, deltas = refs[: 2 * GROUP], refs[2 * GROUP : -7]
    out, keeps_hbm, gives_hbm, keeps, gives, table, sems = refs[-7:]
    quarter, core = place[0], place[1]
    tiles = LANES // units
    samples = hidden.shape[1]
    shard = deltas[0].shape[0]
    for i, delta in enumerate(deltas):
        table[i * shard : (i + 1) * shard] = delta[...]
    low = lane_mask(ROWS, True).astype(jnp.float32).astype(jnp.bfloat16)
    high = lane_mask(ROWS, False).astype(jnp.float32).astype(jnp.bfloat16)
    keep = gene_lanes(samples, tiles)
    row_gene = lax.broadcasted_iota(jnp.int32, (LANES, LANES), 0) % tiles
    lane_gene = lax.broadcasted_iota(jnp.int32, (LANES, LANES), 1) // samples
    fits = [
        (row_gene == lane_gene + i * (LANES // samples)).astype(jnp.float32)
        for i in range(tiles * samples // LANES)
    ]
    copies = []
    for index in range(2 * GROUP):
        piece = index % GROUP
        grads = gives if index // GROUP else keeps
        source = quarter ^ piece
        half = core ^ (index // GROUP)

        def body(t, _, index=index, piece=piece, grads=grads, source=source, half=half):
            first = half * half_genes + t * tiles
            at = pl.multiple_of(first * units, LANES)
            here = pl.multiple_of(t * LANES, LANES)
            own = hidden[source, :, pl.ds(at, LANES)].astype(jnp.float32)
            gene = source * (2 * half_genes) + first
            parts = []
            for r in range(tiles):
                one = table[slots[members[0, gene + r]]]
                two = table[slots[members[1, gene + r]]]
                parts.append(one * low + swap_halves(two) * high)
                parts.append(swap_halves(one) * low + two * high)
            right = jnp.concatenate(parts, axis=0)
            wide = nt_dot(right, weights[index][pl.ds(here, LANES), :])
            back = wide[:samples] * keep[0]
            for r in range(1, tiles):
                back += wide[r * samples : (r + 1) * samples] * keep[r]
            out[source, :, pl.ds(at, LANES)] = (back * (1.0 - own * own)).astype(out.dtype)
            flat = jnp.concatenate([own] * (LANES // samples), axis=0).T
            left = jnp.concatenate([(flat * fit).astype(jnp.bfloat16) for fit in fits], axis=1)
            grads[piece, pl.ds(here, LANES), :] = nn_dot(left, right).astype(grads.dtype)
            return 0

        lax.fori_loop(0, half_genes // tiles, body, 0, unroll=UNROLL)
        count = head.shape[0] // (2 * GROUP)
        lines = head[pl.ds(pl.multiple_of((2 * source + half) * count, count), count), :]
        coarse = lines.astype(grads.dtype).astype(jnp.float32)
        lines = jnp.concatenate([coarse, lines - coarse], axis=0)
        grads[piece, half_genes * units :, :] = lines.astype(grads.dtype)
        target = gives_hbm if index // GROUP else keeps_hbm
        copies.append(pltpu.make_async_copy(grads.at[piece], target.at[piece], sems.at[index]))
        copies[-1].start()
    for copy in copies:
        copy.wait()


def link_backward(place, members, slots, hidden, head, weights, deltas, units):
    rows = hidden.shape[2] // 2
    extra = head.shape[0] // GROUP
    grads = jax.ShapeDtypeStruct((GROUP, rows + extra, LANES), jnp.bfloat16)
    operands = [*weights, *deltas]
    return pl.pallas_call(
        functools.partial(link_backward_kernel, rows // units, units),
        out_shape=[jax.ShapeDtypeStruct(hidden.shape, jnp.bfloat16), grads, grads],
        in_specs=[smem, smem, smem] + [vmem] * (2 + len(operands)),
        out_specs=[vmem, hbm, hbm],
        scratch_shapes=[
            pltpu.VMEM(grads.shape, grads.dtype),
            pltpu.VMEM(grads.shape, grads.dtype),
            pltpu.VMEM((slots.shape[0], ROWS, LANES), jnp.bfloat16),
            pltpu.SemaphoreType.DMA((2 * GROUP,)),
        ],
        compiler_params=pltpu.CompilerParams(vmem_limit_bytes=56 * MIB),
        cost_estimate=pl.CostEstimate(
            flops=6 * 10**9, bytes_accessed=20 * 10**6, transcendentals=0
        ),
        name="link_backward",
    )(place, members, slots, hidden, head, *operands)


def on_device(
    genotypes,
    gene_weight,
    gene_lengths,
    membership,
    pathway_slot,
    pathway_weight,
    head_weight,
    cotangent,
):
    devices = lax.axis_size("genes")
    index = lax.axis_index("genes")
    core = lax.axis_index("batch")
    planes = devices // GROUP
    plane, quarter = index // GROUP, index % GROUP
    gene_count = gene_lengths.shape[0]
    units = gene_weight.shape[0]
    path_units = pathway_weight.shape[1] // units
    slot_count = pathway_slot.shape[0]
    shard = slot_count // planes
    samples = genotypes.shape[0]
    part = samples // GROUP
    in_plane = [[GROUP * z + q for q in range(GROUP)] for z in range(planes)]
    along = [[GROUP * z + q for z in range(planes)] for q in range(GROUP)]
    paired = planes == 4

    def swap_plane(x, d):
        pairs = [(GROUP * z + q, GROUP * z + (q ^ d)) for z in range(planes) for q in range(GROUP)]
        return lax.ppermute(x, "genes", pairs)

    def swap_along(x, d):
        pairs = [(GROUP * z + q, GROUP * (z ^ d) + q) for z in range(planes) for q in range(GROUP)]
        return lax.ppermute(x, "genes", pairs)

    def swap_core(x):
        return lax.ppermute(x, "batch", [(0, 1), (1, 0)])

    def spread(x, groups):
        return lax.all_to_all(
            x, "genes", split_axis=0, concat_axis=0, tiled=True, axis_index_groups=groups
        )

    def after(x, *others):
        return lax.optimization_barrier((x, *others))[0]

    with jax.named_scope("link_weights"):
        head_rows = head_weight.reshape(-1, LANES)
        mine = fold_links(pathway_weight, head_rows, core[None].astype(jnp.int32), units)
        near = [mine] + [swap_plane(mine, d) for d in range(1, GROUP)]

    with jax.named_scope("hidden"):
        hidden = gene_forward(genotypes, gene_weight, gene_lengths)
        other_raw, hidden = lax.optimization_barrier((pathway_weight, hidden))
        hidden = spread(hidden.reshape(GROUP, part, gene_count * units), in_plane)

    with jax.named_scope("link_weights"):
        other = fold_links(other_raw, head_rows, (1 - core)[None].astype(jnp.int32), units)
        far = [other] + [swap_core(x) for x in near[1:]]

    with jax.named_scope("tables"):
        place = jnp.stack([quarter, core]).astype(jnp.int32)
        members = lax.dynamic_slice_in_dim(
            membership, plane * GROUP * gene_count, GROUP * gene_count
        ).T
        slots = pathway_slot ^ (plane * shard) if paired else pathway_slot
        heads = jnp.stack([x[-head_rows.shape[0] :] for x in near])
        head = jnp.concatenate(
            [lax.dynamic_slice_in_dim(heads, quarter ^ d, 1) for d in range(GROUP)]
        )
        head = head.reshape(shard, 1, 1, path_units).astype(jnp.float32)
        cot = lax.dynamic_slice_in_dim(cotangent, quarter * part, part)
        cot = cot.reshape(part // ROWS, ROWS).T.reshape(1, ROWS, part // ROWS, 1)

    def head_step(total, head):
        count = total.shape[0]
        active = jnp.tanh(total.reshape(count, ROWS, part // ROWS, path_units))
        delta = (cot * head * (1.0 - active * active)).astype(jnp.bfloat16)
        return jnp.sum(active * cot, axis=(1, 2)), delta.reshape(count, ROWS, LANES)

    if paired:
        cuts = 2
        count = shard // cuts
        with jax.named_scope("pathway_sum"):
            sums = link_forward(
                place, members, slots, hidden, near + far, planes * cuts, units
            )
            passed = [
                sums[2 * cuts + c].astype(jnp.float32)
                + swap_along(sums[3 * cuts + c], 1).astype(jnp.float32)
                for c in range(cuts)
            ]
            passed = [x.astype(jnp.bfloat16) for x in passed]
            crossed = [swap_along(x, 2) for x in passed]
            beside = [swap_along(after(sums[cuts + c], passed[c]), 1) for c in range(cuts)]
        own, heads = [], []
        for c in range(cuts):
            with jax.named_scope("head"):
                across = after(crossed[c], own[-1]) if c else crossed[c]
                total = (
                    sums[c].astype(jnp.float32)
                    + across.astype(jnp.float32)
                    + beside[c].astype(jnp.float32)
                )
                part_sum, delta = head_step(total, head[c * count : (c + 1) * count])
                own.append(delta)
                heads.append(part_sum)
        head_part = jnp.concatenate(heads)
        with jax.named_scope("pathway_delta"):
            two = [swap_along(x, 2) for x in own]
            one = [swap_along(x, 1) for x in own]
            three = [swap_along(x, 1) for x in two[:-1]] + [swap_along(own[-1], 3)]
            deltas = own + one + two + three
    else:
        with jax.named_scope("pathway_sum"):
            sums = link_forward(place, members, slots, hidden, near + far, planes, units)
            parts = spread(jnp.stack(sums), along)
            total = jnp.sum(parts.astype(jnp.float32), axis=0)
        with jax.named_scope("head"):
            head_part, delta = head_step(total, head)
        with jax.named_scope("pathway_delta"):
            every = lax.all_gather(delta, "genes", axis=0, axis_index_groups=along)
            deltas = [every[i] for i in range(planes)]

    with jax.named_scope("link_grads"):
        head_part = head_part.reshape(-1, LANES)
        extra = head_part.shape[0] // GROUP
        back, keep, give = link_backward(
            place, members, slots, hidden, head_part, near + far, deltas, units
        )
        back = spread(back, in_plane).reshape(samples, gene_count * units)

    with jax.named_scope("grad_pathway"):
        given = swap_core(give)
        summed = [
            (keep[d].astype(jnp.float32) + given[d].astype(jnp.float32)).astype(jnp.bfloat16)
            for d in range(GROUP)
        ]
        parts = [summed[0]] + [swap_plane(summed[d], d) for d in range(1, GROUP)]

    with jax.named_scope("grad_gene"):
        rows = gene_backward(genotypes, back, gene_lengths, units)

    with jax.named_scope("grad_pathway"):
        rows, *parts = lax.optimization_barrier((rows, *parts))
        own = unfold_sum(parts, units, extra)
        grad_gene = rows.astype(jnp.float32) + swap_core(rows).astype(jnp.float32)
        theirs, grad_gene = lax.optimization_barrier((swap_core(own), grad_gene))
        links = pathway_weight.shape[0] // 2
        first = jnp.where(core == 0, own, theirs)
        second = jnp.where(core == 0, theirs, own)
        grad_pathway = jnp.concatenate([first[:links], second[:links]], axis=0)
        width = extra // 2 * LANES
        grad_head = jnp.concatenate([first[links, :width], second[links, :width]])

    return (grad_gene, grad_pathway, grad_head)


def solution(mesh):
    return jax.shard_map(
        on_device,
        mesh=mesh,
        in_specs=(
            P("batch", "genes"),
            P(None, "genes"),
            P("genes"),
            P(),
            P(),
            P("genes", None),
            P("genes"),
            P("batch"),
        ),
        out_specs=(P(None, "genes"), P("genes", None), P("genes")),
        check_vma=False,
    )
```

```python
import functools

import jax
import jax.numpy as jnp
from jax import lax
from jax.experimental import pallas as pl
from jax.experimental.pallas import tpu as pltpu
from jax.sharding import PartitionSpec as P

BLOCK = 512
MIN_GENE = 128
WINDOW = BLOCK // MIN_GENE + 1
GROUP = 4
LANES = 128
ROWS = 16
SUBLANES = 8
UNROLL = 12
MIB = 1024 * 1024

smem = pl.BlockSpec(memory_space=pltpu.SMEM)
vmem = pl.BlockSpec(memory_space=pltpu.VMEM)
hbm = pl.BlockSpec(memory_space=pl.ANY)


def nt_dot(left, right):
    return lax.dot_general(
        left, right, (((1,), (1,)), ((), ())), preferred_element_type=jnp.float32
    )


def nn_dot(left, right):
    return jnp.dot(left, right, preferred_element_type=jnp.float32)


def chunk_blocks(var_count, most):
    total = var_count // BLOCK
    return next(n for n in range(most, 0, -1) if total % n == 0)


def window_edges(lengths, gene_count, gene, start):
    edges = [start]
    for j in range(WINDOW):
        at = gene + j
        length = lengths[jnp.minimum(at, gene_count - 1)]
        edges.append(edges[-1] + jnp.where(at < gene_count, length, 0))
    return edges


def next_window(edges, gene, base):
    start = edges[0]
    for edge in edges[1:]:
        passed = edge <= base
        gene = gene + passed.astype(jnp.int32)
        start = jnp.where(passed, edge, start)
    return gene, start


def reached(edges, base):
    position = lax.broadcasted_iota(jnp.int32, (SUBLANES, BLOCK), 1)
    return [position >= edge - base for edge in edges]


def gene_forward_kernel(
    gene_count, blocks, lengths, geno_hbm, weight_hbm, out, geno, weight, pre, sems
):
    units = weight.shape[0]
    cols = blocks * BLOCK
    chunks = geno.shape[1] // cols

    def copies(c, start, size):
        at = pl.ds(pl.multiple_of(start, BLOCK), size)
        return (
            pltpu.make_async_copy(geno_hbm.at[:, at], geno.at[:, at], sems.at[0, c]),
            pltpu.make_async_copy(weight_hbm.at[:, at], weight.at[:, at], sems.at[1, c]),
        )

    whole = chunks - 1
    pieces = [blocks // 2, blocks // 4, blocks // 4] if blocks % 4 == 0 else [blocks]
    taper, begin = [], whole * cols
    for c, count in enumerate(pieces):
        taper.append((whole + c, begin, count))
        begin += count * BLOCK
    for c in range(whole):
        for copy in copies(c, c * cols, cols):
            copy.start()
    for c, begin, count in taper:
        for copy in copies(c, begin, count * BLOCK):
            copy.start()
    pre[...] = jnp.zeros_like(pre)

    def chunk(c, first, count, carry):
        gene, start = carry
        for copy in copies(c, first, count * BLOCK):
            copy.wait()
        for i in range(count):
            base = first + i * BLOCK
            at = pl.ds(pl.multiple_of(base, BLOCK), BLOCK)
            edges = window_edges(lengths, gene_count, gene, start)
            marks = reached(edges, base)
            wide = weight[:, at]
            rows = []
            for j in range(WINDOW):
                mark = (marks[j] & ~marks[j + 1]).astype(jnp.float32)
                mark = jnp.concatenate([mark] * (units // SUBLANES), axis=0)
                rows.append(wide * mark.astype(wide.dtype))
            part = nt_dot(jnp.concatenate(rows, axis=0), geno[:, at])
            where = pl.ds(pl.multiple_of(gene * units, units), WINDOW * units)
            pre[where, :] += part
            gene, start = next_window(edges, gene, base + BLOCK)
        return gene, start

    carry = (jnp.int32(0), jnp.int32(0))
    carry = lax.fori_loop(0, whole, lambda c, x: chunk(c, c * cols, blocks, x), carry)
    for c, begin, count in taper:
        carry = chunk(c, begin, count, carry)

    def body(i, _):
        at = pl.multiple_of(i * LANES, LANES)
        tile = jnp.concatenate(
            [pre[pl.ds(at + u, LANES // units, stride=units), :] for u in range(units)], axis=0
        )
        out[:, pl.ds(at, LANES)] = jnp.tanh(tile).T.astype(jnp.bfloat16)
        return 0

    lax.fori_loop(0, gene_count * units // LANES, body, 0, unroll=4)


def gene_forward(genotypes, gene_weight, lengths):
    samples, var_count = genotypes.shape
    units = gene_weight.shape[0]
    gene_count = lengths.shape[0]
    blocks = chunk_blocks(var_count, 16)
    return pl.pallas_call(
        functools.partial(gene_forward_kernel, gene_count, blocks),
        out_shape=jax.ShapeDtypeStruct((samples, gene_count * units), jnp.bfloat16),
        in_specs=[smem, hbm, hbm],
        out_specs=vmem,
        scratch_shapes=[
            pltpu.VMEM(genotypes.shape, jnp.bfloat16),
            pltpu.VMEM(gene_weight.shape, jnp.bfloat16),
            pltpu.VMEM(((gene_count + WINDOW) * units, samples), jnp.float32),
            pltpu.SemaphoreType.DMA((2, var_count // (blocks * BLOCK) + 2)),
        ],
        compiler_params=pltpu.CompilerParams(vmem_limit_bytes=52 * MIB),
        cost_estimate=pl.CostEstimate(
            flops=2 * WINDOW * units * samples * var_count,
            bytes_accessed=2 * (samples + units) * var_count,
            transcendentals=gene_count * units * samples,
        ),
        name="gene_forward",
    )(lengths, genotypes, gene_weight)


def gene_backward_kernel(
    gene_count, blocks, lengths, geno_hbm, delta, out_hbm, geno, out, rows, sems
):
    units = out.shape[0]
    cols = blocks * BLOCK
    chunks = geno.shape[1] // cols

    def chunk_copy(c):
        at = pl.ds(pl.multiple_of(c * cols, cols), cols)
        return pltpu.make_async_copy(geno_hbm.at[:, at], geno.at[:, at], sems.at[0, c])

    def chunk_store(c):
        at = pl.ds(pl.multiple_of(c * cols, cols), cols)
        return pltpu.make_async_copy(out.at[:, at], out_hbm.at[:, at], sems.at[1, c])

    for c in range(chunks):
        chunk_copy(c).start()
    tail = WINDOW * units
    rows[gene_count * units :, :] = jnp.zeros((tail, rows.shape[1]), rows.dtype)

    count = LANES // units

    def body(i, _):
        at = pl.multiple_of(i * LANES, LANES)
        tile = delta[:, pl.ds(at, LANES)].astype(jnp.float32).T
        for u in range(units):
            here = pl.ds(at + u, count, stride=units)
            rows[here, :] = tile[u * count : (u + 1) * count]
        return 0

    lax.fori_loop(0, delta.shape[1] // LANES, body, 0, unroll=4)

    def chunk(c, carry):
        gene, start = carry
        chunk_copy(c).wait()
        for i in range(blocks):
            base = c * cols + i * BLOCK
            at = pl.ds(pl.multiple_of(base, BLOCK), BLOCK)
            edges = window_edges(lengths, gene_count, gene, start)
            marks = reached(edges, base)
            where = pl.ds(pl.multiple_of(gene * units, units), WINDOW * units)
            terms = nn_dot(rows[where, :].astype(jnp.bfloat16), geno[:, at])
            pieces = []
            for u in range(0, units, SUBLANES):
                total = terms[u : u + SUBLANES]
                for j in range(1, WINDOW):
                    here = j * units + u
                    total = jnp.where(marks[j], terms[here : here + SUBLANES], total)
                pieces.append(total)
            out[:, at] = jnp.concatenate(pieces, axis=0).astype(out.dtype)
            gene, start = next_window(edges, gene, base + BLOCK)
        chunk_store(c).start()
        return gene, start

    lax.fori_loop(0, chunks, chunk, (jnp.int32(0), jnp.int32(0)))
    for c in range(chunks):
        chunk_store(c).wait()


def gene_backward(genotypes, delta, lengths, units):
    samples, var_count = genotypes.shape
    gene_count = lengths.shape[0]
    blocks = chunk_blocks(var_count, 8)
    return pl.pallas_call(
        functools.partial(gene_backward_kernel, gene_count, blocks),
        out_shape=jax.ShapeDtypeStruct((units, var_count), jnp.bfloat16),
        in_specs=[smem, hbm, vmem],
        out_specs=hbm,
        scratch_shapes=[
            pltpu.VMEM(genotypes.shape, jnp.bfloat16),
            pltpu.VMEM((units, var_count), jnp.bfloat16),
            pltpu.VMEM(((gene_count + WINDOW) * units, samples), jnp.float32),
            pltpu.SemaphoreType.DMA((2, var_count // (blocks * BLOCK))),
        ],
        compiler_params=pltpu.CompilerParams(vmem_limit_bytes=52 * MIB),
        cost_estimate=pl.CostEstimate(
            flops=2 * WINDOW * units * samples * var_count,
            bytes_accessed=4 * (samples + units) * var_count,
            transcendentals=0,
        ),
        name="gene_backward",
    )(lengths, genotypes, delta)


def lane_mask(rows, low):
    lane = lax.broadcasted_iota(jnp.int32, (rows, LANES), 1)
    return lane < LANES // 2 if low else lane >= LANES // 2


def gene_lanes(rows, tiles):
    lane = lax.broadcasted_iota(jnp.int32, (rows, LANES), 1) % tiles
    return [(lane == r).astype(jnp.float32) for r in range(tiles)]


def swap_halves(x):
    half = LANES // 2
    return jnp.concatenate([x[:, half:], x[:, :half]], axis=1)


def fold_kernel(units, which, raw, head, out, wide):
    rows = wide.shape[1]
    start = pl.multiple_of(which[0] * rows, ROWS)
    for c in range(units // 2):
        lanes = slice(c * LANES, (c + 1) * LANES)
        wide[c] = raw[pl.ds(start, rows), lanes].astype(jnp.float32)
    low = lane_mask(SUBLANES, True)

    def body(t, _):
        for c in range(units // 2):
            one = wide[c, pl.ds(t * ROWS, SUBLANES, stride=2), :]
            two = wide[c, pl.ds(t * ROWS + 1, SUBLANES, stride=2), :]
            even = jnp.where(low, one, swap_halves(two))
            odd = jnp.where(low, swap_halves(one), two)
            both = jnp.concatenate([even, odd], axis=0).astype(out.dtype)
            out[pl.ds(pl.multiple_of(t * LANES + c * ROWS, ROWS), ROWS), :] = both
        return 0

    lax.fori_loop(0, rows // ROWS, body, 0, unroll=2)
    out[out.shape[0] - head.shape[0] :, :] = head[...]


def fold_links(raw, head, which, units):
    links, width = raw.shape
    half = links // 2
    rows = half * width // LANES + head.shape[0]
    return pl.pallas_call(
        functools.partial(fold_kernel, units),
        out_shape=jax.ShapeDtypeStruct((rows, LANES), raw.dtype),
        in_specs=[smem, vmem, vmem],
        out_specs=vmem,
        scratch_shapes=[pltpu.VMEM((width // LANES, half, LANES), jnp.float32)],
        compiler_params=pltpu.CompilerParams(vmem_limit_bytes=8 * MIB),
        cost_estimate=pl.CostEstimate(flops=10**6, bytes_accessed=4 * 10**6, transcendentals=0),
        name="fold_links",
    )(which, raw, head)


def unfold_kernel(units, extra, *refs):
    parts, out, wide = refs[:-2], refs[-2], refs[-1]
    low = lane_mask(SUBLANES, True)
    links = wide.shape[1]

    def body(t, _):
        for c in range(units // 2):
            here = pl.ds(pl.multiple_of(t * LANES + c * ROWS, ROWS), ROWS)
            total = parts[0][here, :].astype(jnp.float32)
            for part in parts[1:]:
                total += part[here, :].astype(jnp.float32)
            even, odd = total[:SUBLANES], total[SUBLANES:]
            one = jnp.where(low, even, swap_halves(odd))
            two = jnp.where(low, swap_halves(even), odd)
            wide[c, pl.ds(t * ROWS, SUBLANES, stride=2), :] = one
            wide[c, pl.ds(t * ROWS + 1, SUBLANES, stride=2), :] = two
        return 0

    lax.fori_loop(0, links // ROWS, body, 0, unroll=2)
    head = sum(part[part.shape[0] - extra :, :].astype(jnp.float32) for part in parts)
    head = head[: extra // 2] + head[extra // 2 :]
    for c in range(units // 2):
        lanes = slice(c * LANES, (c + 1) * LANES)
        out[:links, lanes] = wide[c]
        line = head[c : c + 1] if c < extra // 2 else jnp.zeros((1, LANES), jnp.float32)
        out[links:, lanes] = jnp.broadcast_to(line, (SUBLANES, LANES))


def unfold_sum(parts, units, extra):
    rows = (parts[0].shape[0] - extra) // (units // 2)
    return pl.pallas_call(
        functools.partial(unfold_kernel, units, extra),
        out_shape=jax.ShapeDtypeStruct((rows + SUBLANES, units // 2 * LANES), jnp.float32),
        in_specs=[vmem] * len(parts),
        out_specs=vmem,
        scratch_shapes=[pltpu.VMEM((units // 2, rows, LANES), jnp.float32)],
        compiler_params=pltpu.CompilerParams(vmem_limit_bytes=10 * MIB),
        cost_estimate=pl.CostEstimate(flops=10**6, bytes_accessed=4 * 10**6, transcendentals=0),
        name="unfold_sum",
    )(*parts)


def link_forward_kernel(half_genes, units, place, members, slots, hidden, *refs):
    weights, outs, sums = refs[: 2 * GROUP], refs[2 * GROUP : -2], refs[-2:]
    quarter, core = place[0], place[1]
    tiles = LANES // units
    for total in sums:
        total[...] = jnp.zeros_like(total)
    keep = [k.astype(jnp.bfloat16) for k in gene_lanes(ROWS, tiles)]
    low = lane_mask(LANES, True).astype(jnp.float32).astype(jnp.bfloat16)
    high = lane_mask(LANES, False).astype(jnp.float32).astype(jnp.bfloat16)
    for piece in range(2 * GROUP):
        source = quarter ^ (piece % GROUP)
        half = core ^ (piece // GROUP)

        def body(t, _, piece=piece, source=source, half=half):
            first = half * half_genes + t * tiles
            at = pl.multiple_of(first * units, LANES)
            own = hidden[source, :, pl.ds(at, LANES)]
            upper, lower = own[:ROWS], own[ROWS:]
            left = jnp.concatenate(
                [jnp.concatenate([upper * k, lower * k], axis=1) for k in keep], axis=0
            )
            block = weights[piece][pl.ds(pl.multiple_of(t * LANES, LANES), LANES), :]
            turned = swap_halves(block)
            right = jnp.concatenate(
                [
                    jnp.concatenate([block * low, turned * low], axis=1),
                    jnp.concatenate([turned * high, block * high], axis=1),
                ],
                axis=0,
            )
            message = nn_dot(left, right)
            gene = source * (2 * half_genes) + first
            for r in range(tiles):
                for m in range(2):
                    slot = slots[members[m, gene + r]]
                    sums[m][slot] += message[
                        r * ROWS : (r + 1) * ROWS, m * LANES : (m + 1) * LANES
                    ]
            return 0

        lax.fori_loop(0, half_genes // tiles, body, 0, unroll=UNROLL)
    shard = outs[0].shape[0]
    for i, out in enumerate(outs):
        out[...] = (
            sums[0][i * shard : (i + 1) * shard] + sums[1][i * shard : (i + 1) * shard]
        ).astype(out.dtype)


def link_forward(place, members, slots, hidden, weights, shards, units):
    half_genes = hidden.shape[2] // units // 2
    slot_count = slots.shape[0]
    out = jax.ShapeDtypeStruct((slot_count // shards, ROWS, LANES), jnp.bfloat16)
    return pl.pallas_call(
        functools.partial(link_forward_kernel, half_genes, units),
        out_shape=[out] * shards,
        in_specs=[smem, smem, smem, vmem] + [vmem] * len(weights),
        out_specs=[vmem] * shards,
        scratch_shapes=[pltpu.VMEM((slot_count, ROWS, LANES), jnp.float32)] * 2,
        compiler_params=pltpu.CompilerParams(vmem_limit_bytes=slot_count * ROWS * LANES * 10 + 8 * MIB),
        cost_estimate=pl.CostEstimate(
            flops=4 * 10**9, bytes_accessed=8 * 10**6, transcendentals=0
        ),
        name="link_forward",
    )(place, members, slots, hidden, *weights)


def link_backward_kernel(half_genes, units, place, members, slots, hidden, head, *refs):
    weights, deltas = refs[: 2 * GROUP], refs[2 * GROUP : -7]
    out, keeps_hbm, gives_hbm, keeps, gives, table, sems = refs[-7:]
    quarter, core = place[0], place[1]
    tiles = LANES // units
    samples = hidden.shape[1]
    shard = deltas[0].shape[0]
    for i, delta in enumerate(deltas):
        table[i * shard : (i + 1) * shard] = delta[...]
    low = lane_mask(ROWS, True).astype(jnp.float32).astype(jnp.bfloat16)
    high = lane_mask(ROWS, False).astype(jnp.float32).astype(jnp.bfloat16)
    keep = gene_lanes(samples, tiles)
    row_gene = lax.broadcasted_iota(jnp.int32, (LANES, LANES), 0) % tiles
    lane_gene = lax.broadcasted_iota(jnp.int32, (LANES, LANES), 1) // samples
    fits = [
        (row_gene == lane_gene + i * (LANES // samples)).astype(jnp.float32)
        for i in range(tiles * samples // LANES)
    ]
    copies = []
    for index in range(2 * GROUP):
        piece = index % GROUP
        grads = gives if index // GROUP else keeps
        source = quarter ^ piece
        half = core ^ (index // GROUP)

        def body(t, _, index=index, piece=piece, grads=grads, source=source, half=half):
            first = half * half_genes + t * tiles
            at = pl.multiple_of(first * units, LANES)
            here = pl.multiple_of(t * LANES, LANES)
            own = hidden[source, :, pl.ds(at, LANES)].astype(jnp.float32)
            gene = source * (2 * half_genes) + first
            parts = []
            for r in range(tiles):
                one = table[slots[members[0, gene + r]]]
                two = table[slots[members[1, gene + r]]]
                parts.append(one * low + swap_halves(two) * high)
                parts.append(swap_halves(one) * low + two * high)
            right = jnp.concatenate(parts, axis=0)
            wide = nt_dot(right, weights[index][pl.ds(here, LANES), :])
            back = wide[:samples] * keep[0]
            for r in range(1, tiles):
                back += wide[r * samples : (r + 1) * samples] * keep[r]
            out[source, :, pl.ds(at, LANES)] = (back * (1.0 - own * own)).astype(out.dtype)
            flat = jnp.concatenate([own] * (LANES // samples), axis=0).T
            left = jnp.concatenate([(flat * fit).astype(jnp.bfloat16) for fit in fits], axis=1)
            grads[piece, pl.ds(here, LANES), :] = nn_dot(left, right).astype(grads.dtype)
            return 0

        lax.fori_loop(0, half_genes // tiles, body, 0, unroll=UNROLL)
        count = head.shape[0] // (2 * GROUP)
        lines = head[pl.ds(pl.multiple_of((2 * source + half) * count, count), count), :]
        coarse = lines.astype(grads.dtype).astype(jnp.float32)
        lines = jnp.concatenate([coarse, lines - coarse], axis=0)
        grads[piece, half_genes * units :, :] = lines.astype(grads.dtype)
        target = gives_hbm if index // GROUP else keeps_hbm
        copies.append(pltpu.make_async_copy(grads.at[piece], target.at[piece], sems.at[index]))
        copies[-1].start()
    for copy in copies:
        copy.wait()


def link_backward(place, members, slots, hidden, head, weights, deltas, units):
    rows = hidden.shape[2] // 2
    extra = head.shape[0] // GROUP
    grads = jax.ShapeDtypeStruct((GROUP, rows + extra, LANES), jnp.bfloat16)
    operands = [*weights, *deltas]
    return pl.pallas_call(
        functools.partial(link_backward_kernel, rows // units, units),
        out_shape=[jax.ShapeDtypeStruct(hidden.shape, jnp.bfloat16), grads, grads],
        in_specs=[smem, smem, smem] + [vmem] * (2 + len(operands)),
        out_specs=[vmem, hbm, hbm],
        scratch_shapes=[
            pltpu.VMEM(grads.shape, grads.dtype),
            pltpu.VMEM(grads.shape, grads.dtype),
            pltpu.VMEM((slots.shape[0], ROWS, LANES), jnp.bfloat16),
            pltpu.SemaphoreType.DMA((2 * GROUP,)),
        ],
        compiler_params=pltpu.CompilerParams(vmem_limit_bytes=56 * MIB),
        cost_estimate=pl.CostEstimate(
            flops=6 * 10**9, bytes_accessed=20 * 10**6, transcendentals=0
        ),
        name="link_backward",
    )(place, members, slots, hidden, head, *operands)


def on_device(
    genotypes,
    gene_weight,
    gene_lengths,
    membership,
    pathway_slot,
    pathway_weight,
    head_weight,
    cotangent,
):
    devices = lax.axis_size("genes")
    index = lax.axis_index("genes")
    core = lax.axis_index("batch")
    planes = devices // GROUP
    plane, quarter = index // GROUP, index % GROUP
    gene_count = gene_lengths.shape[0]
    units = gene_weight.shape[0]
    path_units = pathway_weight.shape[1] // units
    slot_count = pathway_slot.shape[0]
    shard = slot_count // planes
    samples = genotypes.shape[0]
    part = samples // GROUP
    in_plane = [[GROUP * z + q for q in range(GROUP)] for z in range(planes)]
    along = [[GROUP * z + q for z in range(planes)] for q in range(GROUP)]
    paired = planes == 4

    def swap_plane(x, d):
        pairs = [(GROUP * z + q, GROUP * z + (q ^ d)) for z in range(planes) for q in range(GROUP)]
        return lax.ppermute(x, "genes", pairs)

    def swap_along(x, d):
        pairs = [(GROUP * z + q, GROUP * (z ^ d) + q) for z in range(planes) for q in range(GROUP)]
        return lax.ppermute(x, "genes", pairs)

    def swap_core(x):
        return lax.ppermute(x, "batch", [(0, 1), (1, 0)])

    def spread(x, groups):
        return lax.all_to_all(
            x, "genes", split_axis=0, concat_axis=0, tiled=True, axis_index_groups=groups
        )

    def after(x, *others):
        return lax.optimization_barrier((x, *others))[0]

    with jax.named_scope("link_weights"):
        head_rows = head_weight.reshape(-1, LANES)
        mine = fold_links(pathway_weight, head_rows, core[None].astype(jnp.int32), units)
        near = [mine] + [swap_plane(mine, d) for d in range(1, GROUP)]

    with jax.named_scope("hidden"):
        hidden = gene_forward(genotypes, gene_weight, gene_lengths)
        other_raw, hidden = lax.optimization_barrier((pathway_weight, hidden))
        hidden = spread(hidden.reshape(GROUP, part, gene_count * units), in_plane)

    with jax.named_scope("link_weights"):
        other = fold_links(other_raw, head_rows, (1 - core)[None].astype(jnp.int32), units)
        far = [other] + [swap_core(x) for x in near[1:]]

    with jax.named_scope("tables"):
        place = jnp.stack([quarter, core]).astype(jnp.int32)
        members = lax.dynamic_slice_in_dim(
            membership, plane * GROUP * gene_count, GROUP * gene_count
        ).T
        slots = pathway_slot ^ (plane * shard) if paired else pathway_slot
        heads = jnp.stack([x[-head_rows.shape[0] :] for x in near])
        head = jnp.concatenate(
            [lax.dynamic_slice_in_dim(heads, quarter ^ d, 1) for d in range(GROUP)]
        )
        head = head.reshape(shard, 1, 1, path_units).astype(jnp.float32)
        cot = lax.dynamic_slice_in_dim(cotangent, quarter * part, part)
        cot = cot.reshape(part // ROWS, ROWS).T.reshape(1, ROWS, part // ROWS, 1)

    def head_step(total, head):
        count = total.shape[0]
        active = jnp.tanh(total.reshape(count, ROWS, part // ROWS, path_units))
        delta = (cot * head * (1.0 - active * active)).astype(jnp.bfloat16)
        return jnp.sum(active * cot, axis=(1, 2)), delta.reshape(count, ROWS, LANES)

    if paired:
        cuts = 2
        count = shard // cuts
        with jax.named_scope("pathway_sum"):
            sums = link_forward(
                place, members, slots, hidden, near + far, planes * cuts, units
            )
            passed = [
                sums[2 * cuts + c].astype(jnp.float32)
                + swap_along(sums[3 * cuts + c], 1).astype(jnp.float32)
                for c in range(cuts)
            ]
            passed = [x.astype(jnp.bfloat16) for x in passed]
            crossed = [swap_along(x, 2) for x in passed]
            beside = [swap_along(after(sums[cuts + c], passed[c]), 1) for c in range(cuts)]
        own, heads = [], []
        for c in range(cuts):
            with jax.named_scope("head"):
                across = after(crossed[c], own[-1]) if c else crossed[c]
                total = (
                    sums[c].astype(jnp.float32)
                    + across.astype(jnp.float32)
                    + beside[c].astype(jnp.float32)
                )
                part_sum, delta = head_step(total, head[c * count : (c + 1) * count])
                own.append(delta)
                heads.append(part_sum)
        head_part = jnp.concatenate(heads)
        with jax.named_scope("pathway_delta"):
            two = [swap_along(x, 2) for x in own]
            one = [swap_along(x, 1) for x in own]
            three = [swap_along(x, 1) for x in two[:-1]] + [swap_along(own[-1], 3)]
            deltas = own + one + two + three
    else:
        with jax.named_scope("pathway_sum"):
            sums = link_forward(place, members, slots, hidden, near + far, planes, units)
            parts = spread(jnp.stack(sums), along)
            total = jnp.sum(parts.astype(jnp.float32), axis=0)
        with jax.named_scope("head"):
            head_part, delta = head_step(total, head)
        with jax.named_scope("pathway_delta"):
            every = lax.all_gather(delta, "genes", axis=0, axis_index_groups=along)
            deltas = [every[i] for i in range(planes)]

    with jax.named_scope("link_grads"):
        head_part = head_part.reshape(-1, LANES)
        extra = head_part.shape[0] // GROUP
        back, keep, give = link_backward(
            place, members, slots, hidden, head_part, near + far, deltas, units
        )
        back = spread(back, in_plane).reshape(samples, gene_count * units)

    with jax.named_scope("grad_pathway"):
        given = swap_core(give)
        summed = [
            (keep[d].astype(jnp.float32) + given[d].astype(jnp.float32)).astype(jnp.bfloat16)
            for d in range(GROUP)
        ]
        parts = [summed[0]] + [swap_plane(summed[d], d) for d in range(1, GROUP)]

    with jax.named_scope("grad_gene"):
        rows = gene_backward(genotypes, back, gene_lengths, units)

    with jax.named_scope("grad_pathway"):
        rows, *parts = lax.optimization_barrier((rows, *parts))
        own = unfold_sum(parts, units, extra)
        grad_gene = rows.astype(jnp.float32) + swap_core(rows).astype(jnp.float32)
        theirs, grad_gene = lax.optimization_barrier((swap_core(own), grad_gene))
        links = pathway_weight.shape[0] // 2
        first = jnp.where(core == 0, own, theirs)
        second = jnp.where(core == 0, theirs, own)
        grad_pathway = jnp.concatenate([first[:links], second[:links]], axis=0)
        width = extra // 2 * LANES
        grad_head = jnp.concatenate([first[links, :width], second[links, :width]])

    return (grad_gene, grad_pathway, grad_head)


def solution(mesh):
    return jax.shard_map(
        on_device,
        mesh=mesh,
        in_specs=(
            P("batch", "genes"),
            P(None, "genes"),
            P("genes"),
            P(),
            P(),
            P("genes", None),
            P("genes"),
            P("batch"),
        ),
        out_specs=(P(None, "genes"), P("genes", None), P("genes")),
        check_vma=False,
    )
```

```python
import functools

import jax
import jax.numpy as jnp
from jax import lax
from jax.experimental import pallas as pl
from jax.experimental.pallas import tpu as pltpu
from jax.sharding import PartitionSpec as P

BLOCK = 512
MIN_GENE = 128
WINDOW = BLOCK // MIN_GENE + 1
GROUP = 4
LANES = 128
ROWS = 16
SUBLANES = 8
UNROLL = 12
MIB = 1024 * 1024

smem = pl.BlockSpec(memory_space=pltpu.SMEM)
vmem = pl.BlockSpec(memory_space=pltpu.VMEM)
hbm = pl.BlockSpec(memory_space=pl.ANY)


def nt_dot(left, right):
    return lax.dot_general(
        left, right, (((1,), (1,)), ((), ())), preferred_element_type=jnp.float32
    )


def nn_dot(left, right):
    return jnp.dot(left, right, preferred_element_type=jnp.float32)


def chunk_blocks(var_count, most):
    total = var_count // BLOCK
    return next(n for n in range(most, 0, -1) if total % n == 0)


def window_edges(lengths, gene_count, gene, start):
    edges = [start]
    for j in range(WINDOW):
        at = gene + j
        length = lengths[jnp.minimum(at, gene_count - 1)]
        edges.append(edges[-1] + jnp.where(at < gene_count, length, 0))
    return edges


def next_window(edges, gene, base):
    start = edges[0]
    for edge in edges[1:]:
        passed = edge <= base
        gene = gene + passed.astype(jnp.int32)
        start = jnp.where(passed, edge, start)
    return gene, start


def reached(edges, base):
    position = lax.broadcasted_iota(jnp.int32, (SUBLANES, BLOCK), 1)
    return [position >= edge - base for edge in edges]


def gene_forward_kernel(
    gene_count, blocks, lengths, geno_hbm, weight_hbm, out, geno, weight, pre, sems
):
    units = weight.shape[0]
    cols = blocks * BLOCK
    chunks = geno.shape[1] // cols

    def copies(c, start, size):
        at = pl.ds(pl.multiple_of(start, BLOCK), size)
        return (
            pltpu.make_async_copy(geno_hbm.at[:, at], geno.at[:, at], sems.at[0, c]),
            pltpu.make_async_copy(weight_hbm.at[:, at], weight.at[:, at], sems.at[1, c]),
        )

    whole = chunks - 1
    pieces = [blocks // 2, blocks // 4, blocks // 4] if blocks % 4 == 0 else [blocks]
    taper, begin = [], whole * cols
    for c, count in enumerate(pieces):
        taper.append((whole + c, begin, count))
        begin += count * BLOCK
    for c in range(whole):
        for copy in copies(c, c * cols, cols):
            copy.start()
    for c, begin, count in taper:
        for copy in copies(c, begin, count * BLOCK):
            copy.start()
    pre[...] = jnp.zeros_like(pre)

    def chunk(c, first, count, carry):
        gene, start = carry
        for copy in copies(c, first, count * BLOCK):
            copy.wait()
        for i in range(count):
            base = first + i * BLOCK
            at = pl.ds(pl.multiple_of(base, BLOCK), BLOCK)
            edges = window_edges(lengths, gene_count, gene, start)
            marks = reached(edges, base)
            wide = weight[:, at]
            rows = []
            for j in range(WINDOW):
                mark = (marks[j] & ~marks[j + 1]).astype(jnp.float32)
                mark = jnp.concatenate([mark] * (units // SUBLANES), axis=0)
                rows.append(wide * mark.astype(wide.dtype))
            part = nt_dot(jnp.concatenate(rows, axis=0), geno[:, at])
            where = pl.ds(pl.multiple_of(gene * units, units), WINDOW * units)
            pre[where, :] += part
            gene, start = next_window(edges, gene, base + BLOCK)
        return gene, start

    carry = (jnp.int32(0), jnp.int32(0))
    carry = lax.fori_loop(0, whole, lambda c, x: chunk(c, c * cols, blocks, x), carry)
    for c, begin, count in taper:
        carry = chunk(c, begin, count, carry)

    def body(i, _):
        at = pl.multiple_of(i * LANES, LANES)
        tile = jnp.concatenate(
            [pre[pl.ds(at + u, LANES // units, stride=units), :] for u in range(units)], axis=0
        )
        out[:, pl.ds(at, LANES)] = jnp.tanh(tile).T.astype(jnp.bfloat16)
        return 0

    lax.fori_loop(0, gene_count * units // LANES, body, 0, unroll=4)


def gene_forward(genotypes, gene_weight, lengths):
    samples, var_count = genotypes.shape
    units = gene_weight.shape[0]
    gene_count = lengths.shape[0]
    blocks = chunk_blocks(var_count, 16)
    return pl.pallas_call(
        functools.partial(gene_forward_kernel, gene_count, blocks),
        out_shape=jax.ShapeDtypeStruct((samples, gene_count * units), jnp.bfloat16),
        in_specs=[smem, hbm, hbm],
        out_specs=vmem,
        scratch_shapes=[
            pltpu.VMEM(genotypes.shape, jnp.bfloat16),
            pltpu.VMEM(gene_weight.shape, jnp.bfloat16),
            pltpu.VMEM(((gene_count + WINDOW) * units, samples), jnp.float32),
            pltpu.SemaphoreType.DMA((2, var_count // (blocks * BLOCK) + 2)),
        ],
        compiler_params=pltpu.CompilerParams(vmem_limit_bytes=52 * MIB),
        cost_estimate=pl.CostEstimate(
            flops=2 * WINDOW * units * samples * var_count,
            bytes_accessed=2 * (samples + units) * var_count,
            transcendentals=gene_count * units * samples,
        ),
        name="gene_forward",
    )(lengths, genotypes, gene_weight)


def gene_backward_kernel(
    gene_count, blocks, lengths, geno_hbm, delta, out_hbm, geno, out, rows, sems
):
    units = out.shape[0]
    cols = blocks * BLOCK
    chunks = geno.shape[1] // cols

    def chunk_copy(c):
        at = pl.ds(pl.multiple_of(c * cols, cols), cols)
        return pltpu.make_async_copy(geno_hbm.at[:, at], geno.at[:, at], sems.at[0, c])

    def chunk_store(c):
        at = pl.ds(pl.multiple_of(c * cols, cols), cols)
        return pltpu.make_async_copy(out.at[:, at], out_hbm.at[:, at], sems.at[1, c])

    for c in range(chunks):
        chunk_copy(c).start()
    tail = WINDOW * units
    rows[gene_count * units :, :] = jnp.zeros((tail, rows.shape[1]), rows.dtype)

    count = LANES // units

    def body(i, _):
        at = pl.multiple_of(i * LANES, LANES)
        tile = delta[:, pl.ds(at, LANES)].astype(jnp.float32).T
        for u in range(units):
            here = pl.ds(at + u, count, stride=units)
            rows[here, :] = tile[u * count : (u + 1) * count]
        return 0

    lax.fori_loop(0, delta.shape[1] // LANES, body, 0, unroll=4)

    def chunk(c, carry):
        gene, start = carry
        chunk_copy(c).wait()
        for i in range(blocks):
            base = c * cols + i * BLOCK
            at = pl.ds(pl.multiple_of(base, BLOCK), BLOCK)
            edges = window_edges(lengths, gene_count, gene, start)
            marks = reached(edges, base)
            where = pl.ds(pl.multiple_of(gene * units, units), WINDOW * units)
            terms = nn_dot(rows[where, :].astype(jnp.bfloat16), geno[:, at])
            pieces = []
            for u in range(0, units, SUBLANES):
                total = terms[u : u + SUBLANES]
                for j in range(1, WINDOW):
                    here = j * units + u
                    total = jnp.where(marks[j], terms[here : here + SUBLANES], total)
                pieces.append(total)
            out[:, at] = jnp.concatenate(pieces, axis=0).astype(out.dtype)
            gene, start = next_window(edges, gene, base + BLOCK)
        chunk_store(c).start()
        return gene, start

    lax.fori_loop(0, chunks, chunk, (jnp.int32(0), jnp.int32(0)))
    for c in range(chunks):
        chunk_store(c).wait()


def gene_backward(genotypes, delta, lengths, units):
    samples, var_count = genotypes.shape
    gene_count = lengths.shape[0]
    blocks = chunk_blocks(var_count, 8)
    return pl.pallas_call(
        functools.partial(gene_backward_kernel, gene_count, blocks),
        out_shape=jax.ShapeDtypeStruct((units, var_count), jnp.bfloat16),
        in_specs=[smem, hbm, vmem],
        out_specs=hbm,
        scratch_shapes=[
            pltpu.VMEM(genotypes.shape, jnp.bfloat16),
            pltpu.VMEM((units, var_count), jnp.bfloat16),
            pltpu.VMEM(((gene_count + WINDOW) * units, samples), jnp.float32),
            pltpu.SemaphoreType.DMA((2, var_count // (blocks * BLOCK))),
        ],
        compiler_params=pltpu.CompilerParams(vmem_limit_bytes=52 * MIB),
        cost_estimate=pl.CostEstimate(
            flops=2 * WINDOW * units * samples * var_count,
            bytes_accessed=4 * (samples + units) * var_count,
            transcendentals=0,
        ),
        name="gene_backward",
    )(lengths, genotypes, delta)


def lane_mask(rows, low):
    lane = lax.broadcasted_iota(jnp.int32, (rows, LANES), 1)
    return lane < LANES // 2 if low else lane >= LANES // 2


def gene_lanes(rows, tiles):
    lane = lax.broadcasted_iota(jnp.int32, (rows, LANES), 1) % tiles
    return [(lane == r).astype(jnp.float32) for r in range(tiles)]


def swap_halves(x):
    half = LANES // 2
    return jnp.concatenate([x[:, half:], x[:, :half]], axis=1)


def fold_kernel(units, which, raw, head, out, wide):
    rows = wide.shape[1]
    start = pl.multiple_of(which[0] * rows, ROWS)
    for c in range(units // 2):
        lanes = slice(c * LANES, (c + 1) * LANES)
        wide[c] = raw[pl.ds(start, rows), lanes].astype(jnp.float32)
    low = lane_mask(SUBLANES, True)

    def body(t, _):
        for c in range(units // 2):
            one = wide[c, pl.ds(t * ROWS, SUBLANES, stride=2), :]
            two = wide[c, pl.ds(t * ROWS + 1, SUBLANES, stride=2), :]
            even = jnp.where(low, one, swap_halves(two))
            odd = jnp.where(low, swap_halves(one), two)
            both = jnp.concatenate([even, odd], axis=0).astype(out.dtype)
            out[pl.ds(pl.multiple_of(t * LANES + c * ROWS, ROWS), ROWS), :] = both
        return 0

    lax.fori_loop(0, rows // ROWS, body, 0, unroll=2)
    out[out.shape[0] - head.shape[0] :, :] = head[...]


def fold_links(raw, head, which, units):
    links, width = raw.shape
    half = links // 2
    rows = half * width // LANES + head.shape[0]
    return pl.pallas_call(
        functools.partial(fold_kernel, units),
        out_shape=jax.ShapeDtypeStruct((rows, LANES), raw.dtype),
        in_specs=[smem, vmem, vmem],
        out_specs=vmem,
        scratch_shapes=[pltpu.VMEM((width // LANES, half, LANES), jnp.float32)],
        compiler_params=pltpu.CompilerParams(vmem_limit_bytes=8 * MIB),
        cost_estimate=pl.CostEstimate(flops=10**6, bytes_accessed=4 * 10**6, transcendentals=0),
        name="fold_links",
    )(which, raw, head)


def unfold_kernel(units, extra, *refs):
    parts, out, wide = refs[:-2], refs[-2], refs[-1]
    low = lane_mask(SUBLANES, True)
    links = wide.shape[1]

    def body(t, _):
        for c in range(units // 2):
            here = pl.ds(pl.multiple_of(t * LANES + c * ROWS, ROWS), ROWS)
            total = parts[0][here, :].astype(jnp.float32)
            for part in parts[1:]:
                total += part[here, :].astype(jnp.float32)
            even, odd = total[:SUBLANES], total[SUBLANES:]
            one = jnp.where(low, even, swap_halves(odd))
            two = jnp.where(low, swap_halves(even), odd)
            wide[c, pl.ds(t * ROWS, SUBLANES, stride=2), :] = one
            wide[c, pl.ds(t * ROWS + 1, SUBLANES, stride=2), :] = two
        return 0

    lax.fori_loop(0, links // ROWS, body, 0, unroll=2)
    head = sum(part[part.shape[0] - extra :, :].astype(jnp.float32) for part in parts)
    head = head[: extra // 2] + head[extra // 2 :]
    for c in range(units // 2):
        lanes = slice(c * LANES, (c + 1) * LANES)
        out[:links, lanes] = wide[c]
        line = head[c : c + 1] if c < extra // 2 else jnp.zeros((1, LANES), jnp.float32)
        out[links:, lanes] = jnp.broadcast_to(line, (SUBLANES, LANES))


def unfold_sum(parts, units, extra):
    rows = (parts[0].shape[0] - extra) // (units // 2)
    return pl.pallas_call(
        functools.partial(unfold_kernel, units, extra),
        out_shape=jax.ShapeDtypeStruct((rows + SUBLANES, units // 2 * LANES), jnp.float32),
        in_specs=[vmem] * len(parts),
        out_specs=vmem,
        scratch_shapes=[pltpu.VMEM((units // 2, rows, LANES), jnp.float32)],
        compiler_params=pltpu.CompilerParams(vmem_limit_bytes=10 * MIB),
        cost_estimate=pl.CostEstimate(flops=10**6, bytes_accessed=4 * 10**6, transcendentals=0),
        name="unfold_sum",
    )(*parts)


def link_forward_kernel(half_genes, units, place, members, slots, hidden, *refs):
    weights, outs, sums = refs[: 2 * GROUP], refs[2 * GROUP : -2], refs[-2:]
    quarter, core = place[0], place[1]
    tiles = LANES // units
    for total in sums:
        total[...] = jnp.zeros_like(total)
    keep = [k.astype(jnp.bfloat16) for k in gene_lanes(ROWS, tiles)]
    low = lane_mask(LANES, True).astype(jnp.float32).astype(jnp.bfloat16)
    high = lane_mask(LANES, False).astype(jnp.float32).astype(jnp.bfloat16)
    for piece in range(2 * GROUP):
        source = quarter ^ (piece % GROUP)
        half = core ^ (piece // GROUP)

        def body(t, _, piece=piece, source=source, half=half):
            first = half * half_genes + t * tiles
            at = pl.multiple_of(first * units, LANES)
            own = hidden[source, :, pl.ds(at, LANES)]
            upper, lower = own[:ROWS], own[ROWS:]
            left = jnp.concatenate(
                [jnp.concatenate([upper * k, lower * k], axis=1) for k in keep], axis=0
            )
            block = weights[piece][pl.ds(pl.multiple_of(t * LANES, LANES), LANES), :]
            turned = swap_halves(block)
            right = jnp.concatenate(
                [
                    jnp.concatenate([block * low, turned * low], axis=1),
                    jnp.concatenate([turned * high, block * high], axis=1),
                ],
                axis=0,
            )
            message = nn_dot(left, right)
            gene = source * (2 * half_genes) + first
            for r in range(tiles):
                for m in range(2):
                    slot = slots[members[m, gene + r]]
                    sums[m][slot] += message[
                        r * ROWS : (r + 1) * ROWS, m * LANES : (m + 1) * LANES
                    ]
            return 0

        lax.fori_loop(0, half_genes // tiles, body, 0, unroll=UNROLL)
    shard = outs[0].shape[0]
    for i, out in enumerate(outs):
        out[...] = (
            sums[0][i * shard : (i + 1) * shard] + sums[1][i * shard : (i + 1) * shard]
        ).astype(out.dtype)


def link_forward(place, members, slots, hidden, weights, shards, units):
    half_genes = hidden.shape[2] // units // 2
    slot_count = slots.shape[0]
    out = jax.ShapeDtypeStruct((slot_count // shards, ROWS, LANES), jnp.bfloat16)
    return pl.pallas_call(
        functools.partial(link_forward_kernel, half_genes, units),
        out_shape=[out] * shards,
        in_specs=[smem, smem, smem, vmem] + [vmem] * len(weights),
        out_specs=[vmem] * shards,
        scratch_shapes=[pltpu.VMEM((slot_count, ROWS, LANES), jnp.float32)] * 2,
        compiler_params=pltpu.CompilerParams(vmem_limit_bytes=slot_count * ROWS * LANES * 10 + 8 * MIB),
        cost_estimate=pl.CostEstimate(
            flops=4 * 10**9, bytes_accessed=8 * 10**6, transcendentals=0
        ),
        name="link_forward",
    )(place, members, slots, hidden, *weights)


def link_backward_kernel(half_genes, units, place, members, slots, hidden, head, *refs):
    weights, deltas = refs[: 2 * GROUP], refs[2 * GROUP : -7]
    out, keeps_hbm, gives_hbm, keeps, gives, table, sems = refs[-7:]
    quarter, core = place[0], place[1]
    tiles = LANES // units
    samples = hidden.shape[1]
    shard = deltas[0].shape[0]
    for i, delta in enumerate(deltas):
        table[i * shard : (i + 1) * shard] = delta[...]
    low = lane_mask(ROWS, True).astype(jnp.float32).astype(jnp.bfloat16)
    high = lane_mask(ROWS, False).astype(jnp.float32).astype(jnp.bfloat16)
    keep = gene_lanes(samples, tiles)
    row_gene = lax.broadcasted_iota(jnp.int32, (LANES, LANES), 0) % tiles
    lane_gene = lax.broadcasted_iota(jnp.int32, (LANES, LANES), 1) // samples
    fits = [
        (row_gene == lane_gene + i * (LANES // samples)).astype(jnp.float32)
        for i in range(tiles * samples // LANES)
    ]
    copies = []
    for index in range(2 * GROUP):
        piece = index % GROUP
        grads = gives if index // GROUP else keeps
        source = quarter ^ piece
        half = core ^ (index // GROUP)

        def body(t, _, index=index, piece=piece, grads=grads, source=source, half=half):
            first = half * half_genes + t * tiles
            at = pl.multiple_of(first * units, LANES)
            here = pl.multiple_of(t * LANES, LANES)
            own = hidden[source, :, pl.ds(at, LANES)].astype(jnp.float32)
            gene = source * (2 * half_genes) + first
            parts = []
            for r in range(tiles):
                one = table[slots[members[0, gene + r]]]
                two = table[slots[members[1, gene + r]]]
                parts.append(one * low + swap_halves(two) * high)
                parts.append(swap_halves(one) * low + two * high)
            right = jnp.concatenate(parts, axis=0)
            wide = nt_dot(right, weights[index][pl.ds(here, LANES), :])
            back = wide[:samples] * keep[0]
            for r in range(1, tiles):
                back += wide[r * samples : (r + 1) * samples] * keep[r]
            out[source, :, pl.ds(at, LANES)] = (back * (1.0 - own * own)).astype(out.dtype)
            flat = jnp.concatenate([own] * (LANES // samples), axis=0).T
            left = jnp.concatenate([(flat * fit).astype(jnp.bfloat16) for fit in fits], axis=1)
            grads[piece, pl.ds(here, LANES), :] = nn_dot(left, right).astype(grads.dtype)
            return 0

        lax.fori_loop(0, half_genes // tiles, body, 0, unroll=UNROLL)
        count = head.shape[0] // (2 * GROUP)
        lines = head[pl.ds(pl.multiple_of((2 * source + half) * count, count), count), :]
        coarse = lines.astype(grads.dtype).astype(jnp.float32)
        lines = jnp.concatenate([coarse, lines - coarse], axis=0)
        grads[piece, half_genes * units :, :] = lines.astype(grads.dtype)
        target = gives_hbm if index // GROUP else keeps_hbm
        copies.append(pltpu.make_async_copy(grads.at[piece], target.at[piece], sems.at[index]))
        copies[-1].start()
    for copy in copies:
        copy.wait()


def link_backward(place, members, slots, hidden, head, weights, deltas, units):
    rows = hidden.shape[2] // 2
    extra = head.shape[0] // GROUP
    grads = jax.ShapeDtypeStruct((GROUP, rows + extra, LANES), jnp.bfloat16)
    operands = [*weights, *deltas]
    return pl.pallas_call(
        functools.partial(link_backward_kernel, rows // units, units),
        out_shape=[jax.ShapeDtypeStruct(hidden.shape, jnp.bfloat16), grads, grads],
        in_specs=[smem, smem, smem] + [vmem] * (2 + len(operands)),
        out_specs=[vmem, hbm, hbm],
        scratch_shapes=[
            pltpu.VMEM(grads.shape, grads.dtype),
            pltpu.VMEM(grads.shape, grads.dtype),
            pltpu.VMEM((slots.shape[0], ROWS, LANES), jnp.bfloat16),
            pltpu.SemaphoreType.DMA((2 * GROUP,)),
        ],
        compiler_params=pltpu.CompilerParams(vmem_limit_bytes=53 * MIB),
        cost_estimate=pl.CostEstimate(
            flops=6 * 10**9, bytes_accessed=20 * 10**6, transcendentals=0
        ),
        name="link_backward",
    )(place, members, slots, hidden, head, *operands)


def on_device(
    genotypes,
    gene_weight,
    gene_lengths,
    membership,
    pathway_slot,
    pathway_weight,
    head_weight,
    cotangent,
):
    devices = lax.axis_size("genes")
    index = lax.axis_index("genes")
    core = lax.axis_index("batch")
    planes = devices // GROUP
    plane, quarter = index // GROUP, index % GROUP
    gene_count = gene_lengths.shape[0]
    units = gene_weight.shape[0]
    path_units = pathway_weight.shape[1] // units
    slot_count = pathway_slot.shape[0]
    shard = slot_count // planes
    samples = genotypes.shape[0]
    part = samples // GROUP
    in_plane = [[GROUP * z + q for q in range(GROUP)] for z in range(planes)]
    along = [[GROUP * z + q for z in range(planes)] for q in range(GROUP)]
    paired = planes == 4

    def swap_plane(x, d):
        pairs = [(GROUP * z + q, GROUP * z + (q ^ d)) for z in range(planes) for q in range(GROUP)]
        return lax.ppermute(x, "genes", pairs)

    def swap_along(x, d):
        pairs = [(GROUP * z + q, GROUP * (z ^ d) + q) for z in range(planes) for q in range(GROUP)]
        return lax.ppermute(x, "genes", pairs)

    def swap_core(x):
        return lax.ppermute(x, "batch", [(0, 1), (1, 0)])

    def spread(x, groups):
        return lax.all_to_all(
            x, "genes", split_axis=0, concat_axis=0, tiled=True, axis_index_groups=groups
        )

    def after(x, *others):
        return lax.optimization_barrier((x, *others))[0]

    with jax.named_scope("link_weights"):
        head_rows = head_weight.reshape(-1, LANES)
        mine = fold_links(pathway_weight, head_rows, core[None].astype(jnp.int32), units)
        near = [mine] + [swap_plane(mine, d) for d in range(1, GROUP)]

    with jax.named_scope("hidden"):
        hidden = gene_forward(genotypes, gene_weight, gene_lengths)
        other_raw, hidden = lax.optimization_barrier((pathway_weight, hidden))
        hidden = spread(hidden.reshape(GROUP, part, gene_count * units), in_plane)

    with jax.named_scope("link_weights"):
        other = fold_links(other_raw, head_rows, (1 - core)[None].astype(jnp.int32), units)
        far = [other] + [swap_core(x) for x in near[1:]]

    with jax.named_scope("tables"):
        place = jnp.stack([quarter, core]).astype(jnp.int32)
        members = lax.dynamic_slice_in_dim(
            membership, plane * GROUP * gene_count, GROUP * gene_count
        ).T
        slots = pathway_slot ^ (plane * shard) if paired else pathway_slot
        heads = jnp.stack([x[-head_rows.shape[0] :] for x in near])
        head = jnp.concatenate(
            [lax.dynamic_slice_in_dim(heads, quarter ^ d, 1) for d in range(GROUP)]
        )
        head = head.reshape(shard, 1, 1, path_units).astype(jnp.float32)
        cot = lax.dynamic_slice_in_dim(cotangent, quarter * part, part)
        cot = cot.reshape(part // ROWS, ROWS).T.reshape(1, ROWS, part // ROWS, 1)

    def head_step(total, head):
        count = total.shape[0]
        active = jnp.tanh(total.reshape(count, ROWS, part // ROWS, path_units))
        delta = (cot * head * (1.0 - active * active)).astype(jnp.bfloat16)
        return jnp.sum(active * cot, axis=(1, 2)), delta.reshape(count, ROWS, LANES)

    if paired:
        cuts = 2
        count = shard // cuts
        with jax.named_scope("pathway_sum"):
            sums = link_forward(
                place, members, slots, hidden, near + far, planes * cuts, units
            )
            passed = [
                sums[2 * cuts + c].astype(jnp.float32)
                + swap_along(sums[3 * cuts + c], 1).astype(jnp.float32)
                for c in range(cuts)
            ]
            passed = [x.astype(jnp.bfloat16) for x in passed]
            crossed = [swap_along(x, 2) for x in passed]
            beside = [swap_along(after(sums[cuts + c], passed[c]), 1) for c in range(cuts)]
        own, heads = [], []
        for c in range(cuts):
            with jax.named_scope("head"):
                across = after(crossed[c], own[-1]) if c else crossed[c]
                total = (
                    sums[c].astype(jnp.float32)
                    + across.astype(jnp.float32)
                    + beside[c].astype(jnp.float32)
                )
                part_sum, delta = head_step(total, head[c * count : (c + 1) * count])
                own.append(delta)
                heads.append(part_sum)
        head_part = jnp.concatenate(heads)
        with jax.named_scope("pathway_delta"):
            two = [swap_along(x, 2) for x in own]
            one = [swap_along(x, 1) for x in own]
            three = [swap_along(x, 1) for x in two[:-1]] + [swap_along(own[-1], 3)]
            deltas = own + one + two + three
    else:
        with jax.named_scope("pathway_sum"):
            sums = link_forward(place, members, slots, hidden, near + far, planes, units)
            parts = spread(jnp.stack(sums), along)
            total = jnp.sum(parts.astype(jnp.float32), axis=0)
        with jax.named_scope("head"):
            head_part, delta = head_step(total, head)
        with jax.named_scope("pathway_delta"):
            every = lax.all_gather(delta, "genes", axis=0, axis_index_groups=along)
            deltas = [every[i] for i in range(planes)]

    with jax.named_scope("link_grads"):
        head_part = head_part.reshape(-1, LANES)
        extra = head_part.shape[0] // GROUP
        back, keep, give = link_backward(
            place, members, slots, hidden, head_part, near + far, deltas, units
        )
        back = spread(back, in_plane).reshape(samples, gene_count * units)

    with jax.named_scope("grad_pathway"):
        given = swap_core(give)
        summed = [
            (keep[d].astype(jnp.float32) + given[d].astype(jnp.float32)).astype(jnp.bfloat16)
            for d in range(GROUP)
        ]
        parts = [summed[0]] + [swap_plane(summed[d], d) for d in range(1, GROUP)]

    with jax.named_scope("grad_gene"):
        rows = gene_backward(genotypes, back, gene_lengths, units)

    with jax.named_scope("grad_pathway"):
        rows, *parts = lax.optimization_barrier((rows, *parts))
        own = unfold_sum(parts, units, extra)
        grad_gene = rows.astype(jnp.float32) + swap_core(rows).astype(jnp.float32)
        theirs, grad_gene = lax.optimization_barrier((swap_core(own), grad_gene))
        links = pathway_weight.shape[0] // 2
        first = jnp.where(core == 0, own, theirs)
        second = jnp.where(core == 0, theirs, own)
        grad_pathway = jnp.concatenate([first[:links], second[:links]], axis=0)
        width = extra // 2 * LANES
        grad_head = jnp.concatenate([first[links, :width], second[links, :width]])

    return (grad_gene, grad_pathway, grad_head)


def solution(mesh):
    return jax.shard_map(
        on_device,
        mesh=mesh,
        in_specs=(
            P("batch", "genes"),
            P(None, "genes"),
            P("genes"),
            P(),
            P(),
            P("genes", None),
            P("genes"),
            P("batch"),
        ),
        out_specs=(P(None, "genes"), P("genes", None), P("genes")),
        check_vma=False,
    )
```
